512 devices in a mesh: gx: 32 (over z, x), gy: 16 (over y, core).
Axes of the slice: x: 4, y: 8, z: 8, core: 2. Of those that a mesh axis runs over, the one named last changes fastest.
Arguments:
- iterate: float32 [2, 32, 16, 8, 512], P(None, 'gx', 'gy'), may hold values from -6 to 6
- residual: float32 [2, 32, 16, 8, 512], P(None, 'gx', 'gy'), may hold values from -64 to 64
- direction: float32 [2, 32, 16, 8, 512], P(None, 'gx', 'gy'), may hold values from -64 to 64
- cells: int32 [3, 32, 16, 8, 512], P(None, 'gx', 'gy'), may hold values from 0 to 127, as said below
- fracs: float32 [3, 32, 16, 8, 512], P(None, 'gx', 'gy'), may hold values from 0 to 1
- counts: int32 [32, 16, 8], P('gx', 'gy'), may hold values from 1 to 512, as said below
- slot_tile: int32 [32, 16, 8], P('gx', 'gy'), may hold values from 0 to 7
- spectrum: float32 [256, 256, 256], P('gx', 'gy'), may hold values from 0.2 to 5, as said below
Outputs:
- new_iterate: float32 [2, 32, 16, 8, 512], P(None, 'gx', 'gy')
- new_residual: float32 [2, 32, 16, 8, 512], P(None, 'gx', 'gy')
- new_direction: float32 [2, 32, 16, 8, 512], P(None, 'gx', 'gy')
The draws below stay inside these ranges and needn't reach their ends.
Inputs may be any that keep to these rules, and one draw needn't show every extreme that they name: `cells`: component 0 of a point's cell lies in 16 * t to 16 * t + 15, t being its block's slot_tile; components 1 and 2 lie in the grid pencil of the device that holds the point. `counts`: slots 0 to count - 1 of a block hold live points, the others are padding; on every device some block has 512 live points. Even: spectrum at index (k0, k1, k2) equals spectrum at ((-k0) mod 256, (-k1) mod 256, (-k2) mod 256).
All inputs are finite; a program needn't handle non-finite values.
Results may differ from the reference program's by a relative error of at most 0.0003.
Values sent between devices are 32-bit elements; how exact they have to be, the bound alone decides.
No kernel may reach another device: no remote copies, remote signals or barrier semaphores. Data moves between devices by JAX's collectives and lax.ppermute only.
A program may use at most 64 MiB of HBM per device.

```python
import math
import jax
import jax.numpy as jnp
from jax import lax

G = 128
TL = 16
R = 2
CAP = 512
SLOTS = 8
N_GX = 32
N_GY = 16


def tile_draw(key):
    tile_key = jax.random.fold_in(key, 101)
    return jax.random.randint(tile_key, (N_GX, N_GY, SLOTS), 0, G // TL, dtype=jnp.int32)


def rising():
    dev_pos = (jnp.arange(N_GX)[:, None] * N_GY + jnp.arange(N_GY)[None, :]).astype(jnp.float32)
    dev_pos = dev_pos / max(N_GX * N_GY - 1, 1)
    return (3.0 ** dev_pos)[None, :, :, None, None]


def draw_slot_tile(key, part):
    tiles_drawn = tile_draw(key)
    return tiles_drawn


def draw_cells(key, part):
    tiles_drawn = tile_draw(key)
    key = jax.random.fold_in(key, 5)
    key_depth, key_one, key_two = jax.random.split(key, 3)
    point_shape = (N_GX, N_GY, SLOTS, CAP)
    wide_one = G // N_GX
    wide_two = G // N_GY
    depth = tiles_drawn[..., None] * TL + jax.random.randint(key_depth, point_shape, 0, TL, dtype=jnp.int32)
    start_one = jnp.arange(N_GX, dtype=jnp.int32)[:, None, None, None] * wide_one
    start_two = jnp.arange(N_GY, dtype=jnp.int32)[None, :, None, None] * wide_two
    across = start_one + jax.random.randint(key_one, point_shape, 0, wide_one, dtype=jnp.int32)
    upward = start_two + jax.random.randint(key_two, point_shape, 0, wide_two, dtype=jnp.int32)
    return jnp.stack([depth, across, upward]).astype(jnp.int32)


def draw_counts(key, part):
    key = jax.random.fold_in(key, 7)
    key_base, key_light, key_full = jax.random.split(key, 3)
    block_shape = (N_GX, N_GY, SLOTS)
    base = jax.random.randint(key_base, block_shape, 1, CAP + 1, dtype=jnp.int32)
    light = jax.random.randint(key_light, (N_GX, N_GY, 1), 0, 4, dtype=jnp.int32) > 0
    loaded = jnp.where(light, base // 4 + 1, base)
    full_slot = jax.random.randint(key_full, (N_GX, N_GY, 1), 0, SLOTS, dtype=jnp.int32)
    slot_ids = jnp.arange(SLOTS, dtype=jnp.int32)[None, None, :]
    return jnp.where(slot_ids == full_slot, CAP, loaded).astype(jnp.int32)


def draw_residual(key, part):
    key = jax.random.fold_in(key, 11)
    key_main = jax.random.fold_in(key, 0)
    full_shape = (R, N_GX, N_GY, SLOTS, CAP)
    values = jnp.clip(jax.random.normal(key_main, full_shape, jnp.float32), -6.0, 6.0)
    return values * rising()


def draw_direction(key, part):
    key = jax.random.fold_in(key, 13)
    key_main = jax.random.fold_in(key, 0)
    full_shape = (R, N_GX, N_GY, SLOTS, CAP)
    values = jnp.clip(jax.random.normal(key_main, full_shape, jnp.float32), -6.0, 6.0)
    return values * rising()


def draw_spectrum(key, part):
    key = jax.random.fold_in(key, 17)
    length = 2 * G
    logs = jax.random.uniform(key, (length, length, length), jnp.float32, math.log(0.2), math.log(5.0))
    base = jnp.exp(logs)
    mirrored = jnp.roll(jnp.flip(base, (0, 1, 2)), 1, axis=(0, 1, 2))
    return (0.5 * (base + mirrored)).astype(jnp.float32)


def shard_levels(key, dims, pieces, smallest, largest):
    loudness, own = 1.0, jax.random.fold_in(key, 6)
    for position, blocks in pieces:
        heights = jnp.exp(jax.random.uniform(jax.random.fold_in(own, position), (blocks,), jnp.float32, smallest / len(pieces), largest / len(pieces)))
        loudness = loudness * jnp.repeat(heights, dims[position] // blocks).reshape([-1 if axis == position else 1 for axis in range(len(dims))])
    return loudness


def normal_values(rng, shape, spread, limit, shards=(), held_as=jnp.bfloat16):
    values = spread * jax.random.normal(rng, shape, jnp.float32)
    if shards:
        values = values * shard_levels(rng, shape, shards, -0.22, 0.18)
    return jnp.clip(values, -limit, limit).astype(held_as)


def setup_inputs(seed: int = 0) -> dict:
    key_list = jax.random.split(jax.random.key(seed), 9)
    return {
        "iterate": normal_values(key_list[0], (R, N_GX, N_GY, SLOTS, CAP), 1.0, 6.0, ((1, 32), (2, 16)), jnp.float32),
        "residual": draw_residual(jax.random.fold_in(key_list[8], 71), 0),
        "direction": draw_direction(jax.random.fold_in(key_list[8], 71), 0),
        "cells": draw_cells(jax.random.fold_in(key_list[8], 71), 0),
        "fracs": jnp.clip(1.0 * jax.random.uniform(key_list[4], (3, N_GX, N_GY, SLOTS, CAP), jnp.float32) ** shard_levels(key_list[4], (3, N_GX, N_GY, SLOTS, CAP), ((1, 32), (2, 16)), -0.2, 0.2), 0.0, 1.0),
        "counts": draw_counts(jax.random.fold_in(key_list[8], 71), 0),
        "slot_tile": draw_slot_tile(jax.random.fold_in(key_list[8], 71), 0),
        "spectrum": draw_spectrum(jax.random.fold_in(key_list[8], 71), 0),
    }


noise_var = 0.5
highest = lax.Precision.HIGHEST


def cubic_taps(fraction):
    frac_sq = fraction * fraction
    frac_cube = frac_sq * fraction
    return (-0.5 * frac_cube + frac_sq - 0.5 * fraction,
            1.5 * frac_cube - 2.5 * frac_sq + 1.0,
            -1.5 * frac_cube + 2.0 * frac_sq + 0.5 * fraction,
            0.5 * frac_cube - 0.5 * frac_sq)


def stencil(first_cell, fraction, extent):
    places = lax.broadcasted_iota(jnp.int32, (first_cell.shape[0], extent, first_cell.shape[1]), 1)
    tap_values = cubic_taps(fraction)
    result = jnp.zeros(places.shape, fraction.dtype)
    for offset in range(4):
        result = result + jnp.where(places == (first_cell + offset)[:, None, :], tap_values[offset][:, None, :], 0.0)
    return result


def slot_weights(cell_index, fraction, tile_index, live_mask, start_one, start_two, wide_one, wide_two):
    depth = stencil(cell_index[0] - tile_index[:, None] * TL, fraction[0], TL + 3) * live_mask[:, None, :]
    across = stencil(cell_index[1] - start_one + 1, fraction[1], wide_one + 4)
    upward = stencil(cell_index[2] - start_two + 1, fraction[2], wide_two + 4)
    plane = across[:, :, None, :] * upward[:, None, :, :]
    return depth, plane.reshape(plane.shape[0], (wide_one + 4) * (wide_two + 4), plane.shape[3])


def tile_picks(tile_index, tiles_n):
    return (tile_index[:, None] == jnp.arange(tiles_n, dtype=jnp.int32)[None, :]).astype(jnp.float32)


def reference(iterate, residual, direction, cells, fracs, counts, slot_tile, spectrum):
    wide_one = G // N_GX
    wide_two = G // N_GY
    span = TL + 3
    tiles_n = G // TL
    length = 2 * G
    dev_count = N_GX * N_GY
    probes = direction.shape[0]
    columns = (wide_one + 4) * (wide_two + 4)
    positions = jnp.arange(CAP, dtype=jnp.int32)
    live_mask = (positions[None, None, None, :] < counts[..., None]).astype(jnp.float32)
    masked_dir = direction * live_mask[None]
    masked_res = residual * live_mask[None]
    dev_cells = cells.reshape(3, dev_count, SLOTS, CAP).transpose(1, 0, 2, 3)
    dev_fracs = fracs.reshape(3, dev_count, SLOTS, CAP).transpose(1, 0, 2, 3)
    dev_tiles = slot_tile.reshape(dev_count, SLOTS)
    dev_live = live_mask.reshape(dev_count, SLOTS, CAP)
    dev_dir = masked_dir.reshape(probes, dev_count, SLOTS, CAP).transpose(1, 0, 2, 3)
    dev_ids = jnp.arange(dev_count, dtype=jnp.int32)
    zero_int = jnp.zeros((), jnp.int32)

    def spread_device(grid, item):
        dev_id, cell_index, fraction, tile_index, mask_row, values = item
        start_one = (dev_id // N_GY) * wide_one
        start_two = (dev_id % N_GY) * wide_two
        depth, plane = slot_weights(cell_index, fraction, tile_index, mask_row, start_one, start_two, wide_one, wide_two)
        weighted = depth[None] * values[:, :, None, :]
        contrib = jnp.einsum("rsap,smp->rsam", weighted, plane, precision=highest)
        tile_sums = jnp.einsum("st,rsam->rtam", tile_picks(tile_index, tiles_n), contrib, precision=highest)
        window = jnp.zeros((probes, G + 3, columns), grid.dtype)
        for tile_num in range(tiles_n):
            window = window.at[:, tile_num * TL:tile_num * TL + span].add(tile_sums[:, tile_num])
        window = window.reshape(probes, G + 3, wide_one + 4, wide_two + 4)
        corner = (zero_int, zero_int, start_one, start_two)
        current = lax.dynamic_slice(grid, corner, window.shape)
        return lax.dynamic_update_slice(grid, current + window, corner), None

    grid = jnp.zeros((probes, G + 3, G + 4, G + 4), jnp.float32)
    grid, unused = lax.scan(spread_device, grid, (dev_ids, dev_cells, dev_fracs, dev_tiles, dev_live, dev_dir))
    field = grid[:, 1:G + 1, 2:G + 2, 2:G + 2]
    spectral = jnp.fft.fftn(field, s=(length, length, length), axes=(1, 2, 3))
    smooth = jnp.real(jnp.fft.ifftn(spectral * spectrum[None], axes=(1, 2, 3)))[:, :G, :G, :G].astype(jnp.float32)
    padded = jnp.pad(smooth, ((0, 0), (1, 2), (2, 2), (2, 2)))

    def read_device(item):
        dev_id, cell_index, fraction, tile_index, mask_row = item
        start_one = (dev_id // N_GY) * wide_one
        start_two = (dev_id % N_GY) * wide_two
        depth, plane = slot_weights(cell_index, fraction, tile_index, mask_row, start_one, start_two, wide_one, wide_two)
        corner = (zero_int, zero_int, start_one, start_two)
        window = lax.dynamic_slice(padded, corner, (probes, G + 3, wide_one + 4, wide_two + 4)).reshape(probes, G + 3, columns)
        blocks = jnp.stack([window[:, tile_num * TL:tile_num * TL + span] for tile_num in range(tiles_n)], axis=1)
        picked = jnp.einsum("st,rtam->rsam", tile_picks(tile_index, tiles_n), blocks, precision=highest)
        partial_h = jnp.einsum("rsam,smp->rsap", picked, plane, precision=highest)
        return jnp.sum(partial_h * depth[None], axis=2)

    gathered = lax.map(read_device, (dev_ids, dev_cells, dev_fracs, dev_tiles, dev_live))
    interp = gathered.transpose(1, 0, 2, 3).reshape(probes, N_GX, N_GY, SLOTS, CAP)
    image = interp + noise_var * masked_dir
    old_norm = jnp.sum(masked_res * masked_res, axis=(1, 2, 3, 4))
    curvature = jnp.sum(masked_dir * image, axis=(1, 2, 3, 4))
    alpha = (old_norm / curvature)[:, None, None, None, None]
    new_iterate = iterate * live_mask[None] + alpha * masked_dir
    new_residual = masked_res - alpha * image
    new_norm = jnp.sum(new_residual * new_residual, axis=(1, 2, 3, 4))
    beta = (new_norm / old_norm)[:, None, None, None, None]
    new_direction = new_residual + beta * masked_dir
    return new_iterate, new_residual, new_direction
```

```python
import functools
import math

import jax
import jax.numpy as jnp
import ml_dtypes
import numpy as np
from jax import lax
from jax.experimental import pallas as pl
from jax.experimental.pallas import tpu as pltpu
from jax.sharding import PartitionSpec as P

G = 128
LENGTH = 2 * G
TL = 16
SPAN = 24
NX = 32
NY = 16
WIDE_ONE = G // NX
WIDE_TWO = G // NY
WIN_ONE = WIDE_ONE + 3
WIN_TWO = WIDE_TWO + 3
PAD_ONE = 8
PAD_TWO = 16
K_ONE = LENGTH // NX
K_TWO = LENGTH // NY
PARTS_X = 2 * WIN_ONE
ROWS_X = 10
EXTRA_X = PARTS_X - ROWS_X
HALF = PAD_TWO - WIN_TWO
ROWS_Y = 2 * WIN_TWO
LANES = 128
WIN_ROWS = 144
NOISE = 0.5
VMEM_LIMIT = 24 * 1024 * 1024
f32 = jnp.float32
bf16 = jnp.bfloat16


def rotation(out_index, in_index, sign, scale):
    turns = (np.outer(out_index, in_index) % LENGTH).astype(np.float64)
    angle = turns * (2.0 * math.pi / LENGTH)
    return np.cos(angle) * scale, sign * np.sin(angle) * scale


def complex_table(out_index, out_part, out_ok, in_index, in_part, in_ok, sign, scale):
    real, imag = rotation(out_index, in_index, sign, scale)
    same = out_part[:, None] == in_part[None, :]
    crossed = np.where(out_part[:, None] == 1, imag, -imag)
    table = np.where(same, real, crossed)
    table = np.where(out_ok[:, None] & in_ok[None, :], table, 0.0)
    high = table.astype(ml_dtypes.bfloat16)
    low = (table - high.astype(np.float64)).astype(ml_dtypes.bfloat16)
    return np.concatenate([high, low], axis=0)


def window_index(owner, offset, wide):
    cell = owner * wide + offset - 1
    return cell, (cell >= 0) & (cell < G)


@functools.lru_cache(None)
def tables():
    def grid(*sizes):
        return [part.reshape(-1) for part in np.meshgrid(*[np.arange(size) for size in sizes], indexing="ij")]

    yes = lambda rows: np.ones(rows.shape, bool)
    n1_part, n1 = grid(2, G)
    k1_part, k1_low, k1_owner = grid(2, K_ONE, NX)
    k1 = k1_owner * K_ONE + k1_low
    x_part, x_cell, x_owner = grid(2, WIN_ONE, NX)
    n2, n2_ok = window_index(x_owner, x_cell, WIDE_ONE)
    came = np.concatenate(
        [
            (np.arange(NX)[:, None] + NX * np.arange(ROWS_X)[None, :]).reshape(-1),
            np.arange(NX * ROWS_X, NX * PARTS_X),
        ]
    )
    k2_part, k2_low, k2_owner = grid(2, K_TWO, NY)
    k2 = k2_owner * K_TWO + k2_low
    y_owner, y_cell, y_part = grid(NY, WIN_TWO, 2)
    n3, n3_ok = window_index(y_owner, y_cell, WIDE_TWO)
    k3_part, k3 = grid(2, LENGTH)
    return (
        complex_table(k1, k1_part, yes(k1), n1, n1_part, yes(n1), -1.0, 1.0),
        complex_table(k2, k2_part, yes(k2), n2[came], x_part[came], n2_ok[came], -1.0, 1.0),
        complex_table(k3, k3_part, yes(k3), n3, y_part, n3_ok, -1.0, 1.0),
        complex_table(n3, y_part, n3_ok, k3, k3_part, yes(k3), 1.0, 1.0 / LENGTH),
        complex_table(n2, x_part, n2_ok, k2, k2_part, yes(k2), 1.0, 1.0 / LENGTH),
        complex_table(n1, n1_part, yes(n1), k1, k1_part, yes(k1), 1.0, 1.0 / LENGTH),
    )


def split(value):
    high = value.astype(bf16)
    return high, (value - high.astype(f32)).astype(bf16)


def dot(left, right, dims=((1,), (0,))):
    return lax.dot_general(left, right, (dims, ((), ())), preferred_element_type=f32)


def transform(table_ref, data):
    rows = table_ref.shape[0] // 2
    data_high, data_low = split(data)
    both = dot(table_ref[:rows], jnp.concatenate([data_high, data_low], axis=1))
    return both[:, :LANES] + both[:, LANES:] + dot(table_ref[rows:], data_high)


def exchange(arrays, block):
    lane = lax.broadcasted_iota(jnp.int32, arrays[0].shape, 1)
    step = 1
    while step < len(arrays):
        width = step * block
        low = (lane // width) % 2 == 0
        mixed = list(arrays)
        for place in range(len(arrays)):
            if place & step:
                continue
            first, second = arrays[place], arrays[place | step]
            mixed[place] = jnp.where(low, first, pltpu.roll(second, width, 1))
            mixed[place | step] = jnp.where(low, pltpu.roll(first, LANES - width, 1), second)
        arrays = mixed
        step *= 2
    return arrays


def lane_cell(shape):
    return lax.broadcasted_iota(jnp.int32, shape, 1) % PAD_TWO


def pack(rows):
    cell = lane_cell(rows[0].shape)
    message = list(rows[:ROWS_X])
    for extra, row in enumerate(rows[ROWS_X:]):
        for half in range(2):
            moved = pltpu.roll(row, WIN_TWO - half * HALF, 1)
            place = 2 * extra + half
            message[place] = jnp.where(cell >= WIN_TWO, moved, message[place])
        place = 2 * EXTRA_X
        message[place] = jnp.where(cell == WIN_TWO + extra, pltpu.roll(row, 1 + extra, 1), message[place])
    return message


def unpack(message):
    cell = lane_cell(message[0].shape)
    rows = []
    for extra in range(EXTRA_X):
        row = pltpu.roll(message[2 * EXTRA_X], LANES - 1 - extra, 1)
        for half in (1, 0):
            moved = pltpu.roll(message[2 * extra + half], LANES - WIN_TWO + half * HALF, 1)
            row = jnp.where(cell < (half + 1) * HALF, moved, row)
        rows.append(row)
    return rows


def gather(ref, row, count, stride):
    return ref[pl.ds(row, count, stride=stride), :]


def live_slots(count_ref, shape):
    slot = lax.broadcasted_iota(jnp.int32, shape, 0)
    limit = jnp.zeros(shape, jnp.int32)
    for index in range(shape[0]):
        limit = jnp.where(slot == index, count_ref[0, 0, index], limit)
    return lax.broadcasted_iota(jnp.int32, shape, 1) < limit


def cubic_taps(fraction):
    frac_sq = fraction * fraction
    frac_cube = frac_sq * fraction
    return (
        -0.5 * frac_cube + frac_sq - 0.5 * fraction,
        1.5 * frac_cube - 2.5 * frac_sq + 1.0,
        -1.5 * frac_cube + 2.0 * frac_sq + 0.5 * fraction,
        0.5 * frac_cube - 0.5 * frac_sq,
    )


def stencil(first, taps, slot, extent):
    first_row = first[slot : slot + 1]
    offset = lax.broadcasted_iota(jnp.int32, (extent, first.shape[1]), 0) - first_row
    result = jnp.zeros(offset.shape, f32)
    for index in range(4):
        result = jnp.where(offset == index, taps[index][slot : slot + 1], result)
    return result


def point_weights(cells_ref, fracs_ref):
    firsts = [cells_ref[dim, 0, 0] & (wide - 1) for dim, wide in enumerate((TL, WIDE_ONE, WIDE_TWO))]
    taps = [cubic_taps(fracs_ref[dim, 0, 0]) for dim in range(3)]

    def weights(slot):
        depth = stencil(firsts[0], taps[0], slot, SPAN)
        across = stencil(firsts[1], taps[1], slot, PAD_ONE)
        upward = stencil(firsts[2], taps[2], slot, PAD_TWO)
        plane = across[:, None, :] * upward[None, :, :]
        return depth, plane.reshape(LANES, plane.shape[2])

    return weights


def spread_kernel(*refs):
    outside, refs = refs[:6], refs[6:]
    out_ref, masked_ref, live_ref, depth_ref, plane_high_ref, plane_low_ref, *inside, win_ref, sems = refs
    tile_ref, count_ref, dir_ref, cells_ref, fracs_ref, table_ref = inside
    copies = [pltpu.make_async_copy(far, near, sems.at[at]) for at, (far, near) in enumerate(zip(outside, inside))]
    for copy in copies:
        copy.start()
    win_ref[...] = jnp.zeros_like(win_ref)
    for copy in copies[:5]:
        copy.wait()
    probes, slots = dir_ref.shape[0], dir_ref.shape[3]
    live = live_slots(count_ref, dir_ref.shape[3:])
    live_ref[...] = live.astype(f32)
    masked = [jnp.where(live, dir_ref[probe, 0, 0], 0.0) for probe in range(probes)]
    for probe in range(probes):
        masked_ref[probe] = masked[probe]
    weights = point_weights(cells_ref, fracs_ref)
    for slot in range(slots):
        depth, plane = weights(slot)
        plane_high, plane_low = split(plane)
        depth_ref[slot], plane_high_ref[slot], plane_low_ref[slot] = depth, plane_high, plane_low
        values = jnp.concatenate([depth * masked[probe][slot : slot + 1] for probe in range(probes)], axis=0)
        value_high, value_low = split(values)
        rows = values.shape[0]
        first = dot(jnp.concatenate([value_high, value_low], axis=0), plane_high, ((1,), (1,)))
        total = first[:rows] + first[rows:] + dot(value_high, plane_low, ((1,), (1,)))
        place = pl.ds(pl.multiple_of(tile_ref[0, 0, slot] * TL, TL), SPAN)
        for probe in range(probes):
            win_ref[probe, place, :] += total[probe * SPAN : (probe + 1) * SPAN]
    field = jnp.concatenate([win_ref[0, 1 : G + 1, :], win_ref[1, 1 : G + 1, :]], axis=0)
    for copy in copies[5:]:
        copy.wait()
    columns = transform(table_ref, field)
    rows = []
    for part in range(2):
        start = part * LENGTH
        pieces = [columns[start + low * NX : start + (low + 1) * NX] for low in range(K_ONE)]
        rows += exchange(pieces, PAD_TWO)[:WIN_ONE]
    for row, piece in enumerate(pack(rows)):
        out_ref[pl.ds(row, NX, stride=ROWS_X), :] = piece


def second_kernel(in_ref, table_ref, out_ref):
    extra = unpack([gather(in_ref, row, NX, ROWS_X) for row in range(2 * EXTRA_X + 1)])
    columns = transform(table_ref, jnp.concatenate([in_ref[...], *extra], axis=0))
    for part in range(2):
        start = part * LENGTH
        pieces = [columns[start + low * NY : start + (low + 1) * NY] for low in range(K_TWO)]
        for cell, piece in enumerate(exchange(pieces, 1)[:WIN_TWO]):
            out_ref[pl.ds(2 * cell + part, NY, stride=ROWS_Y), :] = piece


def third_kernel(in_ref, spec_ref, table_ref, back_ref, out_ref):
    columns = transform(table_ref, in_ref[...])
    factor = spec_ref[...].reshape(LANES, LENGTH).T
    scaled = jnp.concatenate([columns[:LENGTH] * factor, columns[LENGTH:] * factor], axis=0)
    out_ref[...] = transform(back_ref, scaled)


def fourth_kernel(in_ref, table_ref, out_ref):
    parts = []
    for part in range(2):
        pieces = [gather(in_ref, 2 * cell + part, NY, ROWS_Y) for cell in range(WIN_TWO)]
        pieces += [jnp.zeros((NY, LANES), f32)] * (K_TWO - WIN_TWO)
        parts += exchange(pieces, 1)
    columns = transform(table_ref, jnp.concatenate(parts, axis=0))
    rows = [columns[row * NX : (row + 1) * NX] for row in range(PARTS_X)]
    for row, piece in enumerate(pack(rows)):
        out_ref[pl.ds(row, NX, stride=ROWS_X), :] = piece


def read_kernel(
    tile_far_ref, in_ref, res_ref, dir_ref, live_ref, depth_ref, plane_high_ref, plane_low_ref, table_ref,
    image_ref, sums_ref, tile_ref, win_ref, sems,
):
    copy = pltpu.make_async_copy(tile_far_ref, tile_ref, sems.at[0])
    copy.start()
    probes, slots = image_ref.shape[:2]
    rows = [gather(in_ref, row, NX, ROWS_X) for row in range(ROWS_X)]
    rows += unpack(rows)
    parts = []
    for part in range(2):
        pieces = rows[part * WIN_ONE : (part + 1) * WIN_ONE]
        pieces += [jnp.zeros((NX, LANES), f32)] * (PAD_ONE - WIN_ONE)
        parts += exchange(pieces, PAD_TWO)
    smooth = transform(table_ref, jnp.concatenate(parts, axis=0))
    win_ref[...] = jnp.zeros_like(win_ref)
    for probe in range(probes):
        win_ref[probe, 1 : G + 1, :] = smooth[probe * G : (probe + 1) * G]
    copy.wait()
    for slot in range(slots):
        place = pl.ds(pl.multiple_of(tile_ref[0, 0, slot] * TL, TL), SPAN)
        block = jnp.concatenate([win_ref[probe, place, :] for probe in range(probes)], axis=0)
        block_high, block_low = split(block)
        high = plane_high_ref[slot]
        rows = block.shape[0]
        first = dot(jnp.concatenate([block_high, block_low], axis=0), high)
        total = first[:rows] + first[rows:] + dot(block_high, plane_low_ref[slot])
        for probe in range(probes):
            image_ref[probe, slot : slot + 1, :] = jnp.sum(
                depth_ref[slot] * total[probe * SPAN : (probe + 1) * SPAN], axis=0, keepdims=True
            )
    sums = []
    live = live_ref[...]
    for probe in range(probes):
        masked_res, masked_dir = live * res_ref[probe, 0, 0], dir_ref[probe]
        image = live * image_ref[probe] + NOISE * masked_dir
        image_ref[probe] = image
        for left, right in (
            (masked_res, masked_res),
            (masked_dir, image),
            (masked_res, image),
            (image, image),
        ):
            line = jnp.sum(left * right, axis=0, keepdims=True)
            sums.append(sum(line[:, at : at + LANES] for at in range(0, line.shape[1], LANES)))
    column = jnp.sum(jnp.concatenate(sums, axis=0), axis=1, keepdims=True)
    shape = (column.shape[0], LANES)
    own = lax.broadcasted_iota(jnp.int32, shape, 0) == lax.broadcasted_iota(jnp.int32, shape, 1)
    row = jnp.sum(jnp.where(own, column, 0.0), axis=0, keepdims=True)
    sums_ref[...] = jnp.broadcast_to(row, sums_ref.shape)


def total_kernel(in_ref, out_ref):
    out_ref[...] = jnp.broadcast_to(jnp.sum(in_ref[...], axis=0, keepdims=True), out_ref.shape)


def update_kernel(sums_ref, image_ref, live_ref, iterate_ref, res_ref, dir_ref, new_iterate_ref, new_res_ref, new_dir_ref):
    sums = jnp.sum(sums_ref[...], axis=0, keepdims=True)
    live = live_ref[...]
    for probe in range(image_ref.shape[0]):
        old_norm, curvature, crossed, squared = (sums[:, 4 * probe + at : 4 * probe + at + 1] for at in range(4))
        alpha = old_norm / curvature
        new_norm = old_norm + alpha * (alpha * squared - 2.0 * crossed)
        beta = new_norm / old_norm
        masked_dir = dir_ref[probe]
        new_res = live * res_ref[probe, 0, 0] - alpha * image_ref[probe]
        new_iterate_ref[probe, 0, 0] = live * iterate_ref[probe, 0, 0] + alpha * masked_dir
        new_res_ref[probe, 0, 0] = new_res
        new_dir_ref[probe, 0, 0] = new_res + beta * masked_dir


def call(kernel, name, outs, operands, far=0, scratch=()):
    operands = [pltpu.with_memory_space_constraint(operand, pltpu.HBM) for operand in operands[:far]] + [*operands[far:]]
    near = len(operands) - far
    outs = [jax.ShapeDtypeStruct(*(out if isinstance(out[0], tuple) else (out, f32))) for out in outs]
    return pl.pallas_call(
        kernel,
        out_shape=outs,
        in_specs=[pl.BlockSpec(memory_space=pltpu.HBM)] * far + [pl.BlockSpec(memory_space=pltpu.VMEM)] * near,
        out_specs=[pl.BlockSpec(memory_space=pltpu.VMEM)] * len(outs),
        scratch_shapes=list(scratch),
        compiler_params=pltpu.CompilerParams(vmem_limit_bytes=VMEM_LIMIT),
        name=name,
    )(*operands)


def across(axis, value):
    rows = value.shape[0]
    sent = value.reshape(rows, 1, LANES)
    return lax.all_to_all(sent, axis, split_axis=0, concat_axis=0, tiled=True).reshape(rows, LANES)


def on_device(iterate, residual, direction, cells, fracs, counts, slot_tile, spectrum):
    first, second, third, third_back, second_back, first_back = tables()
    probes, slots, cap = direction.shape[0], direction.shape[3], direction.shape[4]
    window = pltpu.VMEM((probes, WIN_ROWS, LANES), f32)
    operands = (slot_tile, counts, direction, cells, fracs, first)
    near = [
        (pltpu.SMEM if at < 2 else pltpu.VMEM)(operand.shape, operand.dtype) for at, operand in enumerate(operands)
    ]
    sent, masked, live, depth, plane_high, plane_low = call(
        spread_kernel,
        "spread",
        [
            (NX * ROWS_X, LANES),
            (probes, slots, cap),
            (slots, cap),
            (slots, SPAN, cap),
            ((slots, LANES, cap), bf16),
            ((slots, LANES, cap), bf16),
        ],
        operands,
        far=len(operands),
        scratch=(*near, window, pltpu.SemaphoreType.DMA((len(operands),))),
    )
    came = across("gx", sent)
    (sent,) = call(second_kernel, "second", [(NY * ROWS_Y, LANES)], (came, second))
    came = across("gy", sent)
    (sent,) = call(third_kernel, "third", [(NY * ROWS_Y, LANES)], (came, spectrum, third, third_back))
    came = across("gy", sent)
    (sent,) = call(fourth_kernel, "fourth", [(NX * ROWS_X, LANES)], (came, second_back))
    came = across("gx", sent)
    image, sums = call(
        read_kernel,
        "read",
        [(probes, slots, cap), (NX, LANES)],
        (slot_tile, came, residual, masked, live, depth, plane_high, plane_low, first_back),
        far=1,
        scratch=(near[0], window, pltpu.SemaphoreType.DMA((1,))),
    )
    sums = across("gx", sums)
    (sums,) = call(total_kernel, "total", [(NY, LANES)], (sums,))
    sums = across("gy", sums)
    return tuple(call(update_kernel, "update", [direction.shape] * 3, (sums, image, live, iterate, residual, masked)))


def solution(mesh):
    points = P(None, "gx", "gy", None, None)
    blocks = P("gx", "gy", None)
    return jax.shard_map(
        on_device,
        mesh=mesh,
        in_specs=(points, points, points, points, points, blocks, blocks, blocks),
        out_specs=(points, points, points),
        check_vma=False,
    )
```

```python
import functools
import math

import jax
import jax.numpy as jnp
import ml_dtypes
import numpy as np
from jax import lax
from jax.experimental import pallas as pl
from jax.experimental.pallas import tpu as pltpu
from jax.sharding import PartitionSpec as P

G = 128
LENGTH = 2 * G
TL = 16
SPAN = 24
NX = 32
NY = 16
WIDE_ONE = G // NX
WIDE_TWO = G // NY
WIN_ONE = WIDE_ONE + 3
WIN_TWO = WIDE_TWO + 3
PAD_ONE = 8
PAD_TWO = 16
K_ONE = LENGTH // NX
K_TWO = LENGTH // NY
PARTS_X = 2 * WIN_ONE
ROWS_X = 10
EXTRA_X = PARTS_X - ROWS_X
HALF = PAD_TWO - WIN_TWO
ROWS_Y = 2 * WIN_TWO
LANES = 128
WIN_ROWS = 144
NOISE = 0.5
VMEM_LIMIT = 24 * 1024 * 1024
f32 = jnp.float32
bf16 = jnp.bfloat16


def rotation(out_index, in_index, sign, scale):
    turns = (np.outer(out_index, in_index) % LENGTH).astype(np.float64)
    angle = turns * (2.0 * math.pi / LENGTH)
    return np.cos(angle) * scale, sign * np.sin(angle) * scale


def complex_table(out_index, out_part, out_ok, in_index, in_part, in_ok, sign, scale):
    real, imag = rotation(out_index, in_index, sign, scale)
    same = out_part[:, None] == in_part[None, :]
    crossed = np.where(out_part[:, None] == 1, imag, -imag)
    table = np.where(same, real, crossed)
    table = np.where(out_ok[:, None] & in_ok[None, :], table, 0.0)
    high = table.astype(ml_dtypes.bfloat16)
    low = (table - high.astype(np.float64)).astype(ml_dtypes.bfloat16)
    return np.concatenate([high, low], axis=0)


def window_index(owner, offset, wide):
    cell = owner * wide + offset - 1
    return cell, (cell >= 0) & (cell < G)


@functools.lru_cache(None)
def tables():
    def grid(*sizes):
        return [part.reshape(-1) for part in np.meshgrid(*[np.arange(size) for size in sizes], indexing="ij")]

    yes = lambda rows: np.ones(rows.shape, bool)
    n1_part, n1 = grid(2, G)
    k1_part, k1_low, k1_owner = grid(2, K_ONE, NX)
    k1 = k1_owner * K_ONE + k1_low
    x_part, x_cell, x_owner = grid(2, WIN_ONE, NX)
    n2, n2_ok = window_index(x_owner, x_cell, WIDE_ONE)
    came = np.concatenate(
        [
            (np.arange(NX)[:, None] + NX * np.arange(ROWS_X)[None, :]).reshape(-1),
            np.arange(NX * ROWS_X, NX * PARTS_X),
        ]
    )
    k2_part, k2_low, k2_owner = grid(2, K_TWO, NY)
    k2 = k2_owner * K_TWO + k2_low
    y_owner, y_cell, y_part = grid(NY, WIN_TWO, 2)
    n3, n3_ok = window_index(y_owner, y_cell, WIDE_TWO)
    k3_part, k3 = grid(2, LENGTH)
    return (
        complex_table(k1, k1_part, yes(k1), n1, n1_part, yes(n1), -1.0, 1.0),
        complex_table(k2, k2_part, yes(k2), n2[came], x_part[came], n2_ok[came], -1.0, 1.0),
        complex_table(k3, k3_part, yes(k3), n3, y_part, n3_ok, -1.0, 1.0),
        complex_table(n3, y_part, n3_ok, k3, k3_part, yes(k3), 1.0, 1.0 / LENGTH),
        complex_table(n2, x_part, n2_ok, k2, k2_part, yes(k2), 1.0, 1.0 / LENGTH),
        complex_table(n1, n1_part, yes(n1), k1, k1_part, yes(k1), 1.0, 1.0 / LENGTH),
    )


def split(value):
    high = value.astype(bf16)
    return high, (value - high.astype(f32)).astype(bf16)


def dot(left, right, dims=((1,), (0,))):
    return lax.dot_general(left, right, (dims, ((), ())), preferred_element_type=f32)


def transform(table_ref, data):
    rows = table_ref.shape[0] // 2
    data_high, data_low = split(data)
    both = dot(table_ref[:rows], jnp.concatenate([data_high, data_low], axis=1))
    return both[:, :LANES] + both[:, LANES:] + dot(table_ref[rows:], data_high)


def exchange(arrays, block):
    lane = lax.broadcasted_iota(jnp.int32, arrays[0].shape, 1)
    step = 1
    while step < len(arrays):
        width = step * block
        low = (lane // width) % 2 == 0
        mixed = list(arrays)
        for place in range(len(arrays)):
            if place & step:
                continue
            first, second = arrays[place], arrays[place | step]
            mixed[place] = jnp.where(low, first, pltpu.roll(second, width, 1))
            mixed[place | step] = jnp.where(low, pltpu.roll(first, LANES - width, 1), second)
        arrays = mixed
        step *= 2
    return arrays


def lane_cell(shape):
    return lax.broadcasted_iota(jnp.int32, shape, 1) % PAD_TWO


def pack(rows):
    cell = lane_cell(rows[0].shape)
    message = list(rows[:ROWS_X])
    for extra, row in enumerate(rows[ROWS_X:]):
        for half in range(2):
            moved = pltpu.roll(row, WIN_TWO - half * HALF, 1)
            place = 2 * extra + half
            message[place] = jnp.where(cell >= WIN_TWO, moved, message[place])
        place = 2 * EXTRA_X
        message[place] = jnp.where(cell == WIN_TWO + extra, pltpu.roll(row, 1 + extra, 1), message[place])
    return message


def unpack(message):
    cell = lane_cell(message[0].shape)
    rows = []
    for extra in range(EXTRA_X):
        row = pltpu.roll(message[2 * EXTRA_X], LANES - 1 - extra, 1)
        for half in (1, 0):
            moved = pltpu.roll(message[2 * extra + half], LANES - WIN_TWO + half * HALF, 1)
            row = jnp.where(cell < (half + 1) * HALF, moved, row)
        rows.append(row)
    return rows


def gather(ref, row, count, stride):
    return ref[pl.ds(row, count, stride=stride), :]


def live_slots(count_ref, shape):
    slot = lax.broadcasted_iota(jnp.int32, shape, 0)
    limit = jnp.zeros(shape, jnp.int32)
    for index in range(shape[0]):
        limit = jnp.where(slot == index, count_ref[0, 0, index], limit)
    return lax.broadcasted_iota(jnp.int32, shape, 1) < limit


def cubic_taps(fraction):
    frac_sq = fraction * fraction
    frac_cube = frac_sq * fraction
    return (
        -0.5 * frac_cube + frac_sq - 0.5 * fraction,
        1.5 * frac_cube - 2.5 * frac_sq + 1.0,
        -1.5 * frac_cube + 2.0 * frac_sq + 0.5 * fraction,
        0.5 * frac_cube - 0.5 * frac_sq,
    )


def stencil(first, taps, slot, extent):
    first_row = first[slot : slot + 1]
    offset = lax.broadcasted_iota(jnp.int32, (extent, first.shape[1]), 0) - first_row
    result = jnp.zeros(offset.shape, f32)
    for index in range(4):
        result = jnp.where(offset == index, taps[index][slot : slot + 1], result)
    return result


def point_weights(cells_ref, fracs_ref):
    firsts = [cells_ref[dim, 0, 0] & (wide - 1) for dim, wide in enumerate((TL, WIDE_ONE, WIDE_TWO))]
    taps = [cubic_taps(fracs_ref[dim, 0, 0]) for dim in range(3)]

    def weights(slot):
        depth = stencil(firsts[0], taps[0], slot, SPAN)
        across = stencil(firsts[1], taps[1], slot, PAD_ONE)
        upward = stencil(firsts[2], taps[2], slot, PAD_TWO)
        plane = across[:, None, :] * upward[None, :, :]
        return depth, plane.reshape(LANES, plane.shape[2])

    return weights


def spread_kernel(*refs):
    outside, refs = refs[:6], refs[6:]
    out_ref, masked_ref, live_ref, depth_ref, plane_ref, *inside, win_ref, sems = refs
    tile_ref, count_ref, dir_ref, cells_ref, fracs_ref, table_ref = inside
    copies = [pltpu.make_async_copy(far, near, sems.at[at]) for at, (far, near) in enumerate(zip(outside, inside))]
    for copy in copies:
        copy.start()
    win_ref[...] = jnp.zeros_like(win_ref)
    for copy in copies[:5]:
        copy.wait()
    probes, slots = dir_ref.shape[0], dir_ref.shape[3]
    live = live_slots(count_ref, dir_ref.shape[3:])
    live_ref[...] = live.astype(f32)
    masked = [jnp.where(live, dir_ref[probe, 0, 0], 0.0) for probe in range(probes)]
    for probe in range(probes):
        masked_ref[probe] = masked[probe]
    weights = point_weights(cells_ref, fracs_ref)
    for slot in range(slots):
        depth, plane = weights(slot)
        planes = jnp.concatenate(split(plane), axis=0)
        depth_ref[slot], plane_ref[slot] = depth, planes
        values = jnp.concatenate([depth * masked[probe][slot : slot + 1] for probe in range(probes)], axis=0)
        rows = values.shape[0]
        both = dot(jnp.concatenate(split(values), axis=0), planes, ((1,), (1,)))
        total = both[:rows, :LANES] + (both[:rows, LANES:] + both[rows:, :LANES])
        place = pl.ds(pl.multiple_of(tile_ref[0, 0, slot] * TL, TL), SPAN)
        for probe in range(probes):
            win_ref[probe, place, :] += total[probe * SPAN : (probe + 1) * SPAN]
    field = jnp.concatenate([win_ref[0, 1 : G + 1, :], win_ref[1, 1 : G + 1, :]], axis=0)
    for copy in copies[5:]:
        copy.wait()
    columns = transform(table_ref, field)
    rows = []
    for part in range(2):
        start = part * LENGTH
        pieces = [columns[start + low * NX : start + (low + 1) * NX] for low in range(K_ONE)]
        rows += exchange(pieces, PAD_TWO)[:WIN_ONE]
    for row, piece in enumerate(pack(rows)):
        out_ref[pl.ds(row, NX, stride=ROWS_X), :] = piece


def second_kernel(in_ref, table_ref, out_ref):
    extra = unpack([gather(in_ref, row, NX, ROWS_X) for row in range(2 * EXTRA_X + 1)])
    columns = transform(table_ref, jnp.concatenate([in_ref[...], *extra], axis=0))
    for part in range(2):
        start = part * LENGTH
        pieces = [columns[start + low * NY : start + (low + 1) * NY] for low in range(K_TWO)]
        for cell, piece in enumerate(exchange(pieces, 1)[:WIN_TWO]):
            out_ref[pl.ds(2 * cell + part, NY, stride=ROWS_Y), :] = piece


def third_kernel(in_ref, spec_ref, table_ref, back_ref, out_ref):
    columns = transform(table_ref, in_ref[...])
    factor = spec_ref[...].reshape(LANES, LENGTH).T
    scaled = jnp.concatenate([columns[:LENGTH] * factor, columns[LENGTH:] * factor], axis=0)
    out_ref[...] = transform(back_ref, scaled)


def fourth_kernel(in_ref, table_ref, out_ref):
    parts = []
    for part in range(2):
        pieces = [gather(in_ref, 2 * cell + part, NY, ROWS_Y) for cell in range(WIN_TWO)]
        pieces += [jnp.zeros((NY, LANES), f32)] * (K_TWO - WIN_TWO)
        parts += exchange(pieces, 1)
    columns = transform(table_ref, jnp.concatenate(parts, axis=0))
    rows = [columns[row * NX : (row + 1) * NX] for row in range(PARTS_X)]
    for row, piece in enumerate(pack(rows)):
        out_ref[pl.ds(row, NX, stride=ROWS_X), :] = piece


def read_kernel(
    tile_far_ref, in_ref, res_ref, dir_ref, live_ref, depth_ref, plane_ref, table_ref,
    image_ref, sums_ref, tile_ref, win_ref, sems,
):
    copy = pltpu.make_async_copy(tile_far_ref, tile_ref, sems.at[0])
    copy.start()
    probes, slots = image_ref.shape[:2]
    rows = [gather(in_ref, row, NX, ROWS_X) for row in range(ROWS_X)]
    rows += unpack(rows)
    parts = []
    for part in range(2):
        pieces = rows[part * WIN_ONE : (part + 1) * WIN_ONE]
        pieces += [jnp.zeros((NX, LANES), f32)] * (PAD_ONE - WIN_ONE)
        parts += exchange(pieces, PAD_TWO)
    smooth = transform(table_ref, jnp.concatenate(parts, axis=0))
    win_ref[...] = jnp.zeros_like(win_ref)
    for probe in range(probes):
        win_ref[probe, 1 : G + 1, :] = smooth[probe * G : (probe + 1) * G]
    copy.wait()
    for slot in range(slots):
        place = pl.ds(pl.multiple_of(tile_ref[0, 0, slot] * TL, TL), SPAN)
        block = jnp.concatenate([win_ref[probe, place, :] for probe in range(probes)], axis=0)
        block_high, block_low = split(block)
        rows = block.shape[0]
        left = jnp.concatenate([block_high, block_low], axis=0)
        right = jnp.concatenate([block_high, jnp.zeros_like(block_low)], axis=0)
        both = dot(jnp.concatenate([left, right], axis=1), plane_ref[slot])
        total = both[:rows] + both[rows:]
        for probe in range(probes):
            image_ref[probe, slot : slot + 1, :] = jnp.sum(
                depth_ref[slot] * total[probe * SPAN : (probe + 1) * SPAN], axis=0, keepdims=True
            )
    sums = []
    live = live_ref[...]
    for probe in range(probes):
        masked_res, masked_dir = live * res_ref[probe, 0, 0], dir_ref[probe]
        image = live * image_ref[probe] + NOISE * masked_dir
        image_ref[probe] = image
        for left, right in (
            (masked_res, masked_res),
            (masked_dir, image),
            (masked_res, image),
            (image, image),
        ):
            line = jnp.sum(left * right, axis=0, keepdims=True)
            sums.append(sum(line[:, at : at + LANES] for at in range(0, line.shape[1], LANES)))
    column = jnp.sum(jnp.concatenate(sums, axis=0), axis=1, keepdims=True)
    shape = (column.shape[0], LANES)
    own = lax.broadcasted_iota(jnp.int32, shape, 0) == lax.broadcasted_iota(jnp.int32, shape, 1)
    row = jnp.sum(jnp.where(own, column, 0.0), axis=0, keepdims=True)
    sums_ref[...] = jnp.broadcast_to(row, sums_ref.shape)


def total_kernel(in_ref, out_ref):
    out_ref[...] = jnp.broadcast_to(jnp.sum(in_ref[...], axis=0, keepdims=True), out_ref.shape)


def update_kernel(
    sums_ref, image_ref, live_ref, iterate_ref, res_ref, dir_ref, new_iterate_ref, new_res_ref, new_dir_ref
):
    sums = jnp.sum(sums_ref[...], axis=0, keepdims=True)
    live = live_ref[...]
    for probe in range(image_ref.shape[0]):
        old_norm, curvature, crossed, squared = (sums[:, 4 * probe + at : 4 * probe + at + 1] for at in range(4))
        alpha = old_norm / curvature
        new_norm = old_norm + alpha * (alpha * squared - 2.0 * crossed)
        beta = new_norm / old_norm
        masked_dir = dir_ref[probe]
        new_res = live * res_ref[probe, 0, 0] - alpha * image_ref[probe]
        new_iterate_ref[probe, 0, 0] = live * iterate_ref[probe, 0, 0] + alpha * masked_dir
        new_res_ref[probe, 0, 0] = new_res
        new_dir_ref[probe, 0, 0] = new_res + beta * masked_dir


def call(kernel, name, outs, operands, far=0, scratch=(), cost=None):
    operands = [pltpu.with_memory_space_constraint(operand, pltpu.HBM) for operand in operands[:far]] + [*operands[far:]]
    near = len(operands) - far
    outs = [jax.ShapeDtypeStruct(*(out if isinstance(out[0], tuple) else (out, f32))) for out in outs]
    return pl.pallas_call(
        kernel,
        out_shape=outs,
        in_specs=[pl.BlockSpec(memory_space=pltpu.HBM)] * far + [pl.BlockSpec(memory_space=pltpu.VMEM)] * near,
        out_specs=[pl.BlockSpec(memory_space=pltpu.VMEM)] * len(outs),
        scratch_shapes=list(scratch),
        compiler_params=pltpu.CompilerParams(vmem_limit_bytes=VMEM_LIMIT),
        cost_estimate=cost,
        name=name,
    )(*operands)


def across(axis, value):
    rows = value.shape[0]
    sent = value.reshape(rows, 1, LANES)
    return lax.all_to_all(sent, axis, split_axis=0, concat_axis=0, tiled=True).reshape(rows, LANES)


def on_device(iterate, residual, direction, cells, fracs, counts, slot_tile, spectrum):
    first, second, third, third_back, second_back, first_back = tables()
    probes, slots, cap = direction.shape[0], direction.shape[3], direction.shape[4]
    window = pltpu.VMEM((probes, WIN_ROWS, LANES), f32)
    operands = (slot_tile, counts, direction, cells, fracs, first)
    near = [
        (pltpu.SMEM if at < 2 else pltpu.VMEM)(operand.shape, operand.dtype) for at, operand in enumerate(operands)
    ]
    sent, masked, live, depth, planes = call(
        spread_kernel,
        "spread",
        [
            (NX * ROWS_X, LANES),
            (probes, slots, cap),
            (slots, cap),
            (slots, SPAN, cap),
            ((slots, 2 * LANES, cap), bf16),
        ],
        operands,
        far=len(operands),
        cost=pl.CostEstimate(flops=400_000_000, bytes_accessed=8_000_000, transcendentals=0),
        scratch=(*near, window, pltpu.SemaphoreType.DMA((len(operands),))),
    )
    came = across("gx", sent)
    (sent,) = call(second_kernel, "second", [(NY * ROWS_Y, LANES)], (came, second))
    came = across("gy", sent)
    (sent,) = call(third_kernel, "third", [(NY * ROWS_Y, LANES)], (came, spectrum, third, third_back))
    came = across("gy", sent)
    (sent,) = call(fourth_kernel, "fourth", [(NX * ROWS_X, LANES)], (came, second_back))
    came = across("gx", sent)
    image, sums = call(
        read_kernel,
        "read",
        [(probes, slots, cap), (NX, LANES)],
        (slot_tile, came, residual, masked, live, depth, planes, first_back),
        far=1,
        scratch=(near[0], window, pltpu.SemaphoreType.DMA((1,))),
    )
    sums = across("gx", sums)
    (sums,) = call(total_kernel, "total", [(NY, LANES)], (sums,))
    sums = across("gy", sums)
    return tuple(call(update_kernel, "update", [direction.shape] * 3, (sums, image, live, iterate, residual, masked)))


def solution(mesh):
    points = P(None, "gx", "gy", None, None)
    blocks = P("gx", "gy", None)
    return jax.shard_map(
        on_device,
        mesh=mesh,
        in_specs=(points, points, points, points, points, blocks, blocks, blocks),
        out_specs=(points, points, points),
        check_vma=False,
    )
```

```python
import functools
import math

import jax
import jax.numpy as jnp
import ml_dtypes
import numpy as np
from jax import lax
from jax.experimental import pallas as pl
from jax.experimental.pallas import tpu as pltpu
from jax.sharding import PartitionSpec as P

G = 128
LENGTH = 2 * G
TL = 16
SPAN = 24
NX = 32
NY = 16
WIDE_ONE = G // NX
WIDE_TWO = G // NY
WIN_ONE = WIDE_ONE + 3
WIN_TWO = WIDE_TWO + 3
PAD_ONE = 8
PAD_TWO = 16
K_ONE = LENGTH // NX
K_TWO = LENGTH // NY
PARTS_X = 2 * WIN_ONE
ROWS_X = 10
EXTRA_X = PARTS_X - ROWS_X
HALF = PAD_TWO - WIN_TWO
ROWS_Y = 2 * WIN_TWO
LANES = 128
WIN_ROWS = 144
NOISE = 0.5
VMEM_LIMIT = 24 * 1024 * 1024
f32 = jnp.float32
bf16 = jnp.bfloat16


def rotation(out_index, in_index, sign, scale):
    turns = (np.outer(out_index, in_index) % LENGTH).astype(np.float64)
    angle = turns * (2.0 * math.pi / LENGTH)
    return np.cos(angle) * scale, sign * np.sin(angle) * scale


def table(out_index, out_ok, in_index, in_ok, sign, scale):
    parts = rotation(out_index, in_index, sign, scale)
    values = np.concatenate([np.where(out_ok[:, None] & in_ok[None, :], part, 0.0) for part in parts], axis=0)
    high = values.astype(ml_dtypes.bfloat16)
    low = (values - high.astype(np.float64)).astype(ml_dtypes.bfloat16)
    return np.concatenate([high, low, high], axis=1)


def window_index(owner, offset, wide):
    cell = owner * wide + offset - 1
    return cell, (cell >= 0) & (cell < G)


@functools.lru_cache(None)
def tables():
    def grid(*sizes):
        return [part.reshape(-1) for part in np.meshgrid(*[np.arange(size) for size in sizes], indexing="ij")]

    yes = lambda rows: np.ones(rows.shape, bool)
    n1 = np.arange(G)
    k1_low, k1_owner = grid(K_ONE, NX)
    k1 = k1_owner * K_ONE + k1_low
    x_cell, x_owner = grid(WIN_ONE, NX)
    n2, n2_ok = window_index(x_owner, x_cell, WIDE_ONE)
    k2_low, k2_owner = grid(K_TWO, NY)
    k2 = k2_owner * K_TWO + k2_low
    y_cell, y_owner = grid(WIN_TWO, NY)
    n3, n3_ok = window_index(y_owner, y_cell, WIDE_TWO)
    k3 = np.arange(LENGTH)
    return (
        table(k1, yes(k1), n1, yes(n1), -1.0, 1.0),
        table(k2, yes(k2), n2, n2_ok, -1.0, 1.0),
        table(k3, yes(k3), n3, n3_ok, -1.0, 1.0),
        table(n3, n3_ok, k3, yes(k3), 1.0, 1.0 / LENGTH),
        table(n2, n2_ok, k2, yes(k2), 1.0, 1.0 / LENGTH),
        table(n1, yes(n1), k1, yes(k1), 1.0, 1.0 / LENGTH),
    )


def split(value):
    high = value.astype(bf16)
    return high, (value - high.astype(f32)).astype(bf16)


def dot(left, right, dims=((1,), (0,))):
    return lax.dot_general(left, right, (dims, ((), ())), preferred_element_type=f32)


def transform(table_ref, real, imag):
    high, low = split(jnp.concatenate([real, imag], axis=1))
    data = jnp.concatenate([high, high, low], axis=0)
    rows = table_ref.shape[0] // 2
    cos, sin = dot(table_ref[:rows], data), dot(table_ref[rows:], data)
    return cos[:, :LANES] - sin[:, LANES:], cos[:, LANES:] + sin[:, :LANES]


def exchange(arrays, block):
    lane = lax.broadcasted_iota(jnp.int32, arrays[0].shape, 1)
    step = 1
    while step < len(arrays):
        width = step * block
        low = (lane // width) % 2 == 0
        mixed = list(arrays)
        for place in range(len(arrays)):
            if place & step:
                continue
            first, second = arrays[place], arrays[place | step]
            mixed[place] = jnp.where(low, first, pltpu.roll(second, width, 1))
            mixed[place | step] = jnp.where(low, pltpu.roll(first, LANES - width, 1), second)
        arrays = mixed
        step *= 2
    return arrays


def lane_cell(shape):
    return lax.broadcasted_iota(jnp.int32, shape, 1) % PAD_TWO


def pack(rows):
    cell = lane_cell(rows[0].shape)
    message = list(rows[:ROWS_X])
    for extra, row in enumerate(rows[ROWS_X:]):
        for half in range(2):
            moved = pltpu.roll(row, WIN_TWO - half * HALF, 1)
            place = 2 * extra + half
            message[place] = jnp.where(cell >= WIN_TWO, moved, message[place])
        place = 2 * EXTRA_X
        message[place] = jnp.where(cell == WIN_TWO + extra, pltpu.roll(row, 1 + extra, 1), message[place])
    return message


def unpack(message):
    cell = lane_cell(message[0].shape)
    rows = []
    for extra in range(EXTRA_X):
        row = pltpu.roll(message[2 * EXTRA_X], LANES - 1 - extra, 1)
        for half in (1, 0):
            moved = pltpu.roll(message[2 * extra + half], LANES - WIN_TWO + half * HALF, 1)
            row = jnp.where(cell < (half + 1) * HALF, moved, row)
        rows.append(row)
    return rows


def gather(ref, row, count, stride):
    return ref[pl.ds(row, count, stride=stride), :]


def live_slots(count_ref, shape):
    slot = lax.broadcasted_iota(jnp.int32, shape, 0)
    limit = jnp.zeros(shape, jnp.int32)
    for index in range(shape[0]):
        limit = jnp.where(slot == index, count_ref[0, 0, index], limit)
    return lax.broadcasted_iota(jnp.int32, shape, 1) < limit


def cubic_taps(fraction):
    frac_sq = fraction * fraction
    frac_cube = frac_sq * fraction
    return (
        -0.5 * frac_cube + frac_sq - 0.5 * fraction,
        1.5 * frac_cube - 2.5 * frac_sq + 1.0,
        -1.5 * frac_cube + 2.0 * frac_sq + 0.5 * fraction,
        0.5 * frac_cube - 0.5 * frac_sq,
    )


def stencil(first, taps, slot, extent):
    first_row = first[slot : slot + 1]
    offset = lax.broadcasted_iota(jnp.int32, (extent, first.shape[1]), 0) - first_row
    result = jnp.zeros(offset.shape, f32)
    for index in range(4):
        result = jnp.where(offset == index, taps[index][slot : slot + 1], result)
    return result


def point_weights(cells_ref, fracs_ref):
    firsts = [cells_ref[dim, 0, 0] & (wide - 1) for dim, wide in enumerate((TL, WIDE_ONE, WIDE_TWO))]
    taps = [cubic_taps(fracs_ref[dim, 0, 0]) for dim in range(3)]

    def weights(slot):
        depth = stencil(firsts[0], taps[0], slot, SPAN)
        across = stencil(firsts[1], taps[1], slot, PAD_ONE)
        upward = stencil(firsts[2], taps[2], slot, PAD_TWO)
        plane = across[:, None, :] * upward[None, :, :]
        return depth, plane.reshape(LANES, plane.shape[2])

    return weights


def spread_kernel(*refs):
    outside, refs = refs[:6], refs[6:]
    out_ref, masked_ref, live_ref, depth_ref, plane_ref, *inside, win_ref, sems = refs
    tile_ref, count_ref, dir_ref, cells_ref, fracs_ref, table_ref = inside
    copies = [pltpu.make_async_copy(far, near, sems.at[at]) for at, (far, near) in enumerate(zip(outside, inside))]
    for copy in copies:
        copy.start()
    win_ref[...] = jnp.zeros_like(win_ref)
    for copy in copies[:5]:
        copy.wait()
    probes, slots = dir_ref.shape[0], dir_ref.shape[3]
    live = live_slots(count_ref, dir_ref.shape[3:])
    live_ref[...] = live.astype(f32)
    masked = [jnp.where(live, dir_ref[probe, 0, 0], 0.0) for probe in range(probes)]
    for probe in range(probes):
        masked_ref[probe] = masked[probe]
    weights = point_weights(cells_ref, fracs_ref)
    for slot in range(slots):
        depth, plane = weights(slot)
        planes = jnp.concatenate(split(plane), axis=0)
        depth_ref[slot], plane_ref[slot] = depth, planes
        values = jnp.concatenate([depth * masked[probe][slot : slot + 1] for probe in range(probes)], axis=0)
        rows = values.shape[0]
        both = dot(jnp.concatenate(split(values), axis=0), planes, ((1,), (1,)))
        total = both[:rows, :LANES] + (both[:rows, LANES:] + both[rows:, :LANES])
        place = pl.ds(pl.multiple_of(tile_ref[0, 0, slot] * TL, TL), SPAN)
        for probe in range(probes):
            win_ref[probe, place, :] += total[probe * SPAN : (probe + 1) * SPAN]
    for copy in copies[5:]:
        copy.wait()
    rows = []
    for columns in transform(table_ref, win_ref[0, 1 : G + 1, :], win_ref[1, 1 : G + 1, :]):
        pieces = [columns[low * NX : (low + 1) * NX] for low in range(K_ONE)]
        rows += exchange(pieces, PAD_TWO)[:WIN_ONE]
    for row, piece in enumerate(pack(rows)):
        out_ref[pl.ds(row, NX, stride=ROWS_X), :] = piece


def window_rows(in_ref):
    rows = [gather(in_ref, row, NX, ROWS_X) for row in range(ROWS_X)]
    return rows + unpack(rows)


def second_kernel(in_ref, table_ref, out_ref):
    rows = window_rows(in_ref)
    window = [jnp.concatenate(rows[part * WIN_ONE : (part + 1) * WIN_ONE], axis=0) for part in range(2)]
    for part, columns in enumerate(transform(table_ref, *window)):
        pieces = [columns[low * NY : (low + 1) * NY] for low in range(K_TWO)]
        for cell, piece in enumerate(exchange(pieces, 1)[:WIN_TWO]):
            out_ref[pl.ds(2 * cell + part, NY, stride=ROWS_Y), :] = piece


def third_kernel(in_ref, spec_ref, table_ref, back_ref, out_ref):
    window = [
        jnp.concatenate([gather(in_ref, 2 * cell + part, NY, ROWS_Y) for cell in range(WIN_TWO)], axis=0)
        for part in range(2)
    ]
    factor = spec_ref[...].reshape(LANES, LENGTH).T
    scaled = [columns * factor for columns in transform(table_ref, *window)]
    for part, columns in enumerate(transform(back_ref, *scaled)):
        for cell in range(WIN_TWO):
            out_ref[pl.ds(2 * cell + part, NY, stride=ROWS_Y), :] = columns[cell * NY : (cell + 1) * NY]


def fourth_kernel(in_ref, table_ref, out_ref):
    parts = []
    for part in range(2):
        pieces = [gather(in_ref, 2 * cell + part, NY, ROWS_Y) for cell in range(WIN_TWO)]
        pieces += [jnp.zeros((NY, LANES), f32)] * (K_TWO - WIN_TWO)
        parts.append(jnp.concatenate(exchange(pieces, 1), axis=0))
    rows = []
    for columns in transform(table_ref, *parts):
        rows += [columns[cell * NX : (cell + 1) * NX] for cell in range(WIN_ONE)]
    for row, piece in enumerate(pack(rows)):
        out_ref[pl.ds(row, NX, stride=ROWS_X), :] = piece


def read_kernel(
    tile_far_ref, in_ref, res_ref, dir_ref, live_ref, depth_ref, plane_ref, table_ref,
    image_ref, sums_ref, tile_ref, win_ref, sems,
):
    copy = pltpu.make_async_copy(tile_far_ref, tile_ref, sems.at[0])
    copy.start()
    probes, slots = image_ref.shape[:2]
    rows = window_rows(in_ref)
    parts = []
    for part in range(2):
        pieces = rows[part * WIN_ONE : (part + 1) * WIN_ONE]
        pieces += [jnp.zeros((NX, LANES), f32)] * (PAD_ONE - WIN_ONE)
        parts.append(jnp.concatenate(exchange(pieces, PAD_TWO), axis=0))
    smooth = transform(table_ref, *parts)
    win_ref[...] = jnp.zeros_like(win_ref)
    for probe in range(probes):
        win_ref[probe, 1 : G + 1, :] = smooth[probe]
    copy.wait()
    for slot in range(slots):
        place = pl.ds(pl.multiple_of(tile_ref[0, 0, slot] * TL, TL), SPAN)
        block = jnp.concatenate([win_ref[probe, place, :] for probe in range(probes)], axis=0)
        block_high, block_low = split(block)
        rows = block.shape[0]
        left = jnp.concatenate([block_high, block_low], axis=0)
        right = jnp.concatenate([block_high, jnp.zeros_like(block_low)], axis=0)
        both = dot(jnp.concatenate([left, right], axis=1), plane_ref[slot])
        total = both[:rows] + both[rows:]
        for probe in range(probes):
            image_ref[probe, slot : slot + 1, :] = jnp.sum(
                depth_ref[slot] * total[probe * SPAN : (probe + 1) * SPAN], axis=0, keepdims=True
            )
    sums = []
    live = live_ref[...]
    for probe in range(probes):
        masked_res, masked_dir = live * res_ref[probe, 0, 0], dir_ref[probe]
        image = live * image_ref[probe] + NOISE * masked_dir
        image_ref[probe] = image
        for left, right in (
            (masked_res, masked_res),
            (masked_dir, image),
            (masked_res, image),
            (image, image),
        ):
            line = jnp.sum(left * right, axis=0, keepdims=True)
            sums.append(sum(line[:, at : at + LANES] for at in range(0, line.shape[1], LANES)))
    column = jnp.sum(jnp.concatenate(sums, axis=0), axis=1, keepdims=True)
    shape = (column.shape[0], LANES)
    own = lax.broadcasted_iota(jnp.int32, shape, 0) == lax.broadcasted_iota(jnp.int32, shape, 1)
    row = jnp.sum(jnp.where(own, column, 0.0), axis=0, keepdims=True)
    sums_ref[...] = jnp.broadcast_to(row, sums_ref.shape)


def total_kernel(in_ref, out_ref):
    out_ref[...] = jnp.broadcast_to(jnp.sum(in_ref[...], axis=0, keepdims=True), out_ref.shape)


def update_kernel(
    sums_ref, image_ref, live_ref, iterate_ref, res_ref, dir_ref, new_iterate_ref, new_res_ref, new_dir_ref
):
    sums = jnp.sum(sums_ref[...], axis=0, keepdims=True)
    live = live_ref[...]
    for probe in range(image_ref.shape[0]):
        old_norm, curvature, crossed, squared = (sums[:, 4 * probe + at : 4 * probe + at + 1] for at in range(4))
        alpha = old_norm / curvature
        new_norm = old_norm + alpha * (alpha * squared - 2.0 * crossed)
        beta = new_norm / old_norm
        masked_dir = dir_ref[probe]
        new_res = live * res_ref[probe, 0, 0] - alpha * image_ref[probe]
        new_iterate_ref[probe, 0, 0] = live * iterate_ref[probe, 0, 0] + alpha * masked_dir
        new_res_ref[probe, 0, 0] = new_res
        new_dir_ref[probe, 0, 0] = new_res + beta * masked_dir


def call(kernel, name, outs, operands, far=0, scratch=(), cost=None):
    operands = [pltpu.with_memory_space_constraint(operand, pltpu.HBM) for operand in operands[:far]] + [*operands[far:]]
    near = len(operands) - far
    outs = [jax.ShapeDtypeStruct(*(out if isinstance(out[0], tuple) else (out, f32))) for out in outs]
    return pl.pallas_call(
        kernel,
        out_shape=outs,
        in_specs=[pl.BlockSpec(memory_space=pltpu.HBM)] * far + [pl.BlockSpec(memory_space=pltpu.VMEM)] * near,
        out_specs=[pl.BlockSpec(memory_space=pltpu.VMEM)] * len(outs),
        scratch_shapes=list(scratch),
        compiler_params=pltpu.CompilerParams(vmem_limit_bytes=VMEM_LIMIT),
        cost_estimate=cost,
        name=name,
    )(*operands)


def across(axis, value):
    rows = value.shape[0]
    sent = value.reshape(rows, 1, LANES)
    return lax.all_to_all(sent, axis, split_axis=0, concat_axis=0, tiled=True).reshape(rows, LANES)


def on_device(iterate, residual, direction, cells, fracs, counts, slot_tile, spectrum):
    first, second, third, third_back, second_back, first_back = tables()
    probes, slots, cap = direction.shape[0], direction.shape[3], direction.shape[4]
    window = pltpu.VMEM((probes, WIN_ROWS, LANES), f32)
    operands = (slot_tile, counts, direction, cells, fracs, first)
    near = [
        (pltpu.SMEM if at < 2 else pltpu.VMEM)(operand.shape, operand.dtype) for at, operand in enumerate(operands)
    ]
    sent, masked, live, depth, planes = call(
        spread_kernel,
        "spread",
        [
            (NX * ROWS_X, LANES),
            (probes, slots, cap),
            (slots, cap),
            (slots, SPAN, cap),
            ((slots, 2 * LANES, cap), bf16),
        ],
        operands,
        far=len(operands),
        cost=pl.CostEstimate(flops=400_000_000, bytes_accessed=8_000_000, transcendentals=0),
        scratch=(*near, window, pltpu.SemaphoreType.DMA((len(operands),))),
    )
    came = across("gx", sent)
    (sent,) = call(second_kernel, "second", [(NY * ROWS_Y, LANES)], (came, second))
    came = across("gy", sent)
    (sent,) = call(third_kernel, "third", [(NY * ROWS_Y, LANES)], (came, spectrum, third, third_back))
    came = across("gy", sent)
    (sent,) = call(fourth_kernel, "fourth", [(NX * ROWS_X, LANES)], (came, second_back))
    came = across("gx", sent)
    image, sums = call(
        read_kernel,
        "read",
        [(probes, slots, cap), (NX, LANES)],
        (slot_tile, came, residual, masked, live, depth, planes, first_back),
        far=1,
        scratch=(near[0], window, pltpu.SemaphoreType.DMA((1,))),
    )
    sums = across("gx", sums)
    (sums,) = call(total_kernel, "total", [(NY, LANES)], (sums,))
    sums = across("gy", sums)
    return tuple(call(update_kernel, "update", [direction.shape] * 3, (sums, image, live, iterate, residual, masked)))


def solution(mesh):
    points = P(None, "gx", "gy", None, None)
    blocks = P("gx", "gy", None)
    return jax.shard_map(
        on_device,
        mesh=mesh,
        in_specs=(points, points, points, points, points, blocks, blocks, blocks),
        out_specs=(points, points, points),
        check_vma=False,
    )
```

```python
import functools
import math

import jax
import jax.numpy as jnp
import ml_dtypes
import numpy as np
from jax import lax
from jax.experimental import pallas as pl
from jax.experimental.pallas import tpu as pltpu
from jax.sharding import PartitionSpec as P

G = 128
LENGTH = 2 * G
TL = 16
SPAN = 24
NX = 32
NY = 16
WIDE_ONE = G // NX
WIDE_TWO = G // NY
WIN_ONE = WIDE_ONE + 3
WIN_TWO = WIDE_TWO + 3
PAD_ONE = 8
PAD_TWO = 16
K_ONE = LENGTH // NX
K_TWO = LENGTH // NY
PARTS_X = 2 * WIN_ONE
ROWS_X = 10
EXTRA_X = PARTS_X - ROWS_X
HALF = PAD_TWO - WIN_TWO
ROWS_Y = 2 * WIN_TWO
LANES = 128
WIN_ROWS = 144
NOISE = 0.5
VMEM_LIMIT = 24 * 1024 * 1024
f32 = jnp.float32
bf16 = jnp.bfloat16


def rotation(out_index, in_index, sign, scale):
    turns = (np.outer(out_index, in_index) % LENGTH).astype(np.float64)
    angle = turns * (2.0 * math.pi / LENGTH)
    return np.cos(angle) * scale, sign * np.sin(angle) * scale


def table(out_index, out_ok, in_index, in_ok, sign, scale):
    parts = rotation(out_index, in_index, sign, scale)
    values = np.concatenate([np.where(out_ok[:, None] & in_ok[None, :], part, 0.0) for part in parts], axis=0)
    high = values.astype(ml_dtypes.bfloat16)
    low = (values - high.astype(np.float64)).astype(ml_dtypes.bfloat16)
    return np.concatenate([high, low, high], axis=1)


def window_index(owner, offset, wide):
    cell = owner * wide + offset - 1
    return cell, (cell >= 0) & (cell < G)


@functools.lru_cache(None)
def tables():
    def grid(*sizes):
        return [part.reshape(-1) for part in np.meshgrid(*[np.arange(size) for size in sizes], indexing="ij")]

    yes = lambda rows: np.ones(rows.shape, bool)
    n1 = np.arange(G)
    k1_low, k1_owner = grid(K_ONE, NX)
    k1 = k1_owner * K_ONE + k1_low
    x_cell, x_owner = grid(WIN_ONE, NX)
    n2, n2_ok = window_index(x_owner, x_cell, WIDE_ONE)
    k2_low, k2_owner = grid(K_TWO, NY)
    k2 = k2_owner * K_TWO + k2_low
    y_cell, y_owner = grid(WIN_TWO, NY)
    n3, n3_ok = window_index(y_owner, y_cell, WIDE_TWO)
    k3 = np.arange(LENGTH)
    return (
        table(k1, yes(k1), n1, yes(n1), -1.0, 1.0),
        table(k2, yes(k2), n2, n2_ok, -1.0, 1.0),
        table(k3, yes(k3), n3, n3_ok, -1.0, 1.0),
        table(n3, n3_ok, k3, yes(k3), 1.0, 1.0 / LENGTH),
        table(n2, n2_ok, k2, yes(k2), 1.0, 1.0 / LENGTH),
        table(n1, yes(n1), k1, yes(k1), 1.0, 1.0 / LENGTH),
    )


def split(value):
    high = value.astype(bf16)
    return high, (value - high.astype(f32)).astype(bf16)


def dot(left, right, dims=((1,), (0,))):
    return lax.dot_general(left, right, (dims, ((), ())), preferred_element_type=f32)


def transform(table_ref, real, imag):
    high, low = split(jnp.concatenate([real, imag], axis=1))
    data = jnp.concatenate([high, high, low], axis=0)
    rows = table_ref.shape[0] // 2
    cos, sin = dot(table_ref[:rows], data), dot(table_ref[rows:], data)
    return cos[:, :LANES] - sin[:, LANES:], cos[:, LANES:] + sin[:, :LANES]


def exchange(arrays, block):
    lane = lax.broadcasted_iota(jnp.int32, arrays[0].shape, 1)
    step = 1
    while step < len(arrays):
        width = step * block
        low = (lane // width) % 2 == 0
        mixed = list(arrays)
        for place in range(len(arrays)):
            if place & step:
                continue
            first, second = arrays[place], arrays[place | step]
            mixed[place] = jnp.where(low, first, pltpu.roll(second, width, 1))
            mixed[place | step] = jnp.where(low, pltpu.roll(first, LANES - width, 1), second)
        arrays = mixed
        step *= 2
    return arrays


def lane_cell(shape):
    return lax.broadcasted_iota(jnp.int32, shape, 1) % PAD_TWO


def pack(rows):
    cell = lane_cell(rows[0].shape)
    message = list(rows[:ROWS_X])
    for extra, row in enumerate(rows[ROWS_X:]):
        for half in range(2):
            moved = pltpu.roll(row, WIN_TWO - half * HALF, 1)
            place = 2 * extra + half
            message[place] = jnp.where(cell >= WIN_TWO, moved, message[place])
        place = 2 * EXTRA_X
        message[place] = jnp.where(cell == WIN_TWO + extra, pltpu.roll(row, 1 + extra, 1), message[place])
    return message


def unpack(message):
    cell = lane_cell(message[0].shape)
    rows = []
    for extra in range(EXTRA_X):
        row = pltpu.roll(message[2 * EXTRA_X], LANES - 1 - extra, 1)
        for half in (1, 0):
            moved = pltpu.roll(message[2 * extra + half], LANES - WIN_TWO + half * HALF, 1)
            row = jnp.where(cell < (half + 1) * HALF, moved, row)
        rows.append(row)
    return rows


def gather(ref, row, count, stride):
    return ref[pl.ds(row, count, stride=stride), :]


def live_slots(count_ref, shape):
    slot = lax.broadcasted_iota(jnp.int32, shape, 0)
    limit = jnp.zeros(shape, jnp.int32)
    for index in range(shape[0]):
        limit = jnp.where(slot == index, count_ref[0, 0, index], limit)
    return lax.broadcasted_iota(jnp.int32, shape, 1) < limit


def cubic_taps(fraction):
    frac_sq = fraction * fraction
    frac_cube = frac_sq * fraction
    return (
        -0.5 * frac_cube + frac_sq - 0.5 * fraction,
        1.5 * frac_cube - 2.5 * frac_sq + 1.0,
        -1.5 * frac_cube + 2.0 * frac_sq + 0.5 * fraction,
        0.5 * frac_cube - 0.5 * frac_sq,
    )


def stencil(first, taps, slot, extent):
    first_row = first[slot : slot + 1]
    offset = lax.broadcasted_iota(jnp.int32, (extent, first.shape[1]), 0) - first_row
    result = jnp.zeros(offset.shape, f32)
    for index in range(4):
        result = jnp.where(offset == index, taps[index][slot : slot + 1], result)
    return result


def point_weights(cells_ref, fracs_ref):
    firsts = [cells_ref[dim, 0, 0] & (wide - 1) for dim, wide in enumerate((TL, WIDE_ONE, WIDE_TWO))]
    taps = [cubic_taps(fracs_ref[dim, 0, 0]) for dim in range(3)]

    def weights(slot):
        depth = stencil(firsts[0], taps[0], slot, SPAN)
        across = stencil(firsts[1], taps[1], slot, PAD_ONE)
        upward = stencil(firsts[2], taps[2], slot, PAD_TWO)
        plane = across[:, None, :] * upward[None, :, :]
        return depth, plane.reshape(LANES, plane.shape[2])

    return weights


def spread_kernel(*refs):
    outside, refs = refs[:6], refs[6:]
    out_ref, masked_ref, live_ref, depth_ref, plane_ref, *inside, win_ref, sems = refs
    tile_ref, count_ref, dir_ref, cells_ref, fracs_ref, table_ref = inside
    copies = [pltpu.make_async_copy(far, near, sems.at[at]) for at, (far, near) in enumerate(zip(outside, inside))]
    for copy in copies:
        copy.start()
    win_ref[...] = jnp.zeros_like(win_ref)
    for copy in copies[:5]:
        copy.wait()
    probes, slots = dir_ref.shape[0], dir_ref.shape[3]
    live = live_slots(count_ref, dir_ref.shape[3:])
    live_ref[...] = live.astype(f32)
    masked = [jnp.where(live, dir_ref[probe, 0, 0], 0.0) for probe in range(probes)]
    for probe in range(probes):
        masked_ref[probe] = masked[probe]
    weights = point_weights(cells_ref, fracs_ref)
    for slot in range(slots):
        depth, plane = weights(slot)
        planes = jnp.concatenate(split(plane), axis=0)
        depth_ref[slot], plane_ref[slot] = depth, planes
        values = jnp.concatenate([depth * masked[probe][slot : slot + 1] for probe in range(probes)], axis=0)
        rows = values.shape[0]
        both = dot(jnp.concatenate(split(values), axis=0), planes, ((1,), (1,)))
        total = both[:rows, :LANES] + (both[:rows, LANES:] + both[rows:, :LANES])
        place = pl.ds(pl.multiple_of(tile_ref[0, 0, slot] * TL, TL), SPAN)
        for probe in range(probes):
            win_ref[probe, place, :] += total[probe * SPAN : (probe + 1) * SPAN]
    for copy in copies[5:]:
        copy.wait()
    rows = []
    for columns in transform(table_ref, win_ref[0, 1 : G + 1, :], win_ref[1, 1 : G + 1, :]):
        pieces = [columns[low * NX : (low + 1) * NX] for low in range(K_ONE)]
        rows += exchange(pieces, PAD_TWO)[:WIN_ONE]
    for row, piece in enumerate(pack(rows)):
        out_ref[pl.ds(row, NX, stride=ROWS_X), :] = piece


def window_rows(in_ref):
    rows = [gather(in_ref, row, NX, ROWS_X) for row in range(ROWS_X)]
    return rows + unpack(rows)


def second_kernel(in_ref, table_ref, out_ref):
    rows = window_rows(in_ref)
    window = [jnp.concatenate(rows[part * WIN_ONE : (part + 1) * WIN_ONE], axis=0) for part in range(2)]
    for part, columns in enumerate(transform(table_ref, *window)):
        pieces = [columns[low * NY : (low + 1) * NY] for low in range(K_TWO)]
        for cell, piece in enumerate(exchange(pieces, 1)[:WIN_TWO]):
            out_ref[pl.ds(2 * cell + part, NY, stride=ROWS_Y), :] = piece


def third_kernel(in_ref, spec_ref, table_ref, back_ref, out_ref):
    window = [
        jnp.concatenate([gather(in_ref, 2 * cell + part, NY, ROWS_Y) for cell in range(WIN_TWO)], axis=0)
        for part in range(2)
    ]
    factor = spec_ref[...].reshape(LANES, LENGTH).T
    scaled = [columns * factor for columns in transform(table_ref, *window)]
    for part, columns in enumerate(transform(back_ref, *scaled)):
        for cell in range(WIN_TWO):
            out_ref[pl.ds(2 * cell + part, NY, stride=ROWS_Y), :] = columns[cell * NY : (cell + 1) * NY]


def fourth_kernel(in_ref, table_ref, out_ref):
    parts = []
    for part in range(2):
        pieces = [gather(in_ref, 2 * cell + part, NY, ROWS_Y) for cell in range(WIN_TWO)]
        pieces += [jnp.zeros((NY, LANES), f32)] * (K_TWO - WIN_TWO)
        parts.append(jnp.concatenate(exchange(pieces, 1), axis=0))
    rows = []
    for columns in transform(table_ref, *parts):
        rows += [columns[cell * NX : (cell + 1) * NX] for cell in range(WIN_ONE)]
    for row, piece in enumerate(pack(rows)):
        out_ref[pl.ds(row, NX, stride=ROWS_X), :] = piece


def read_kernel(
    tile_far_ref, in_ref, res_ref, dir_ref, live_ref, depth_ref, plane_ref, table_ref,
    image_ref, sums_ref, tile_ref, win_ref, sems,
):
    copy = pltpu.make_async_copy(tile_far_ref, tile_ref, sems.at[0])
    copy.start()
    probes, slots = image_ref.shape[:2]
    rows = window_rows(in_ref)
    parts = []
    for part in range(2):
        pieces = rows[part * WIN_ONE : (part + 1) * WIN_ONE]
        pieces += [jnp.zeros((NX, LANES), f32)] * (PAD_ONE - WIN_ONE)
        parts.append(jnp.concatenate(exchange(pieces, PAD_TWO), axis=0))
    smooth = transform(table_ref, *parts)
    win_ref[...] = jnp.zeros_like(win_ref)
    for probe in range(probes):
        win_ref[probe, 1 : G + 1, :] = smooth[probe]
    copy.wait()
    for slot in range(slots):
        place = pl.ds(pl.multiple_of(tile_ref[0, 0, slot] * TL, TL), SPAN)
        block = jnp.concatenate([win_ref[probe, place, :] for probe in range(probes)], axis=0)
        block_high, block_low = split(block)
        rows = block.shape[0]
        left = jnp.concatenate([block_high, block_low], axis=0)
        right = jnp.concatenate([block_high, jnp.zeros_like(block_low)], axis=0)
        both = dot(jnp.concatenate([left, right], axis=1), plane_ref[slot])
        total = both[:rows] + both[rows:]
        for probe in range(probes):
            image_ref[probe, slot : slot + 1, :] = jnp.sum(
                depth_ref[slot] * total[probe * SPAN : (probe + 1) * SPAN], axis=0, keepdims=True
            )
    sums = []
    live = live_ref[...]
    for probe in range(probes):
        masked_res, masked_dir = live * res_ref[probe, 0, 0], dir_ref[probe]
        image = live * image_ref[probe] + NOISE * masked_dir
        image_ref[probe] = image
        for left, right in (
            (masked_res, masked_res),
            (masked_dir, image),
            (masked_res, image),
            (image, image),
        ):
            line = jnp.sum(left * right, axis=0, keepdims=True)
            sums.append(sum(line[:, at : at + LANES] for at in range(0, line.shape[1], LANES)))
    column = jnp.sum(jnp.concatenate(sums, axis=0), axis=1, keepdims=True)
    shape = (column.shape[0], LANES)
    own = lax.broadcasted_iota(jnp.int32, shape, 0) == lax.broadcasted_iota(jnp.int32, shape, 1)
    row = jnp.sum(jnp.where(own, column, 0.0), axis=0, keepdims=True)
    sums_ref[...] = jnp.broadcast_to(row, sums_ref.shape)


def total_kernel(in_ref, out_ref):
    out_ref[...] = jnp.broadcast_to(jnp.sum(in_ref[...], axis=0, keepdims=True), out_ref.shape)


def update_kernel(
    sums_ref, image_ref, live_ref, iterate_ref, res_ref, dir_ref, new_iterate_ref, new_res_ref, new_dir_ref
):
    sums = jnp.sum(sums_ref[...], axis=0, keepdims=True)
    live = live_ref[...]
    for probe in range(image_ref.shape[0]):
        old_norm, curvature, crossed, squared = (sums[:, 4 * probe + at : 4 * probe + at + 1] for at in range(4))
        alpha = old_norm / curvature
        new_norm = old_norm + alpha * (alpha * squared - 2.0 * crossed)
        beta = new_norm / old_norm
        masked_dir = dir_ref[probe]
        new_res = live * res_ref[probe, 0, 0] - alpha * image_ref[probe]
        new_iterate_ref[probe, 0, 0] = live * iterate_ref[probe, 0, 0] + alpha * masked_dir
        new_res_ref[probe, 0, 0] = new_res
        new_dir_ref[probe, 0, 0] = new_res + beta * masked_dir


def call(kernel, name, outs, operands, far=0, scratch=(), cost=None):
    operands = [pltpu.with_memory_space_constraint(operand, pltpu.HBM) for operand in operands[:far]] + [*operands[far:]]
    near = len(operands) - far
    outs = [jax.ShapeDtypeStruct(*(out if isinstance(out[0], tuple) else (out, f32))) for out in outs]
    return pl.pallas_call(
        kernel,
        out_shape=outs,
        in_specs=[pl.BlockSpec(memory_space=pltpu.HBM)] * far + [pl.BlockSpec(memory_space=pltpu.VMEM)] * near,
        out_specs=[pl.BlockSpec(memory_space=pltpu.VMEM)] * len(outs),
        scratch_shapes=list(scratch),
        compiler_params=pltpu.CompilerParams(vmem_limit_bytes=VMEM_LIMIT),
        cost_estimate=cost,
        name=name,
    )(*operands)


def across(axis, value):
    rows = value.shape[0]
    sent = value.reshape(rows, 1, LANES)
    return lax.all_to_all(sent, axis, split_axis=0, concat_axis=0, tiled=True).reshape(rows, LANES)


def on_device(iterate, residual, direction, cells, fracs, counts, slot_tile, spectrum):
    first, second, third, third_back, second_back, first_back = tables()
    probes, slots, cap = direction.shape[0], direction.shape[3], direction.shape[4]
    window = pltpu.VMEM((probes, WIN_ROWS, LANES), f32)
    operands = (slot_tile, counts, direction, cells, fracs, first)
    near = [
        (pltpu.SMEM if at < 2 else pltpu.VMEM)(operand.shape, operand.dtype) for at, operand in enumerate(operands)
    ]
    sent, masked, live, depth, planes = call(
        spread_kernel,
        "spread",
        [
            (NX * ROWS_X, LANES),
            (probes, slots, cap),
            (slots, cap),
            (slots, SPAN, cap),
            ((slots, 2 * LANES, cap), bf16),
        ],
        operands,
        far=len(operands),
        cost=pl.CostEstimate(flops=400_000_000, bytes_accessed=8_000_000, transcendentals=0),
        scratch=(*near, window, pltpu.SemaphoreType.DMA((len(operands),))),
    )
    came = across("gx", sent)
    (sent,) = call(second_kernel, "second", [(NY * ROWS_Y, LANES)], (came, second))
    came = across("gy", sent)
    (sent,) = call(third_kernel, "third", [(NY * ROWS_Y, LANES)], (came, spectrum, third, third_back))
    came = across("gy", sent)
    (sent,) = call(fourth_kernel, "fourth", [(NX * ROWS_X, LANES)], (came, second_back))
    came = across("gx", sent)
    image, sums = call(
        read_kernel,
        "read",
        [(probes, slots, cap), (NY, LANES)],
        (slot_tile, came, residual, masked, live, depth, planes, first_back),
        far=1,
        scratch=(near[0], window, pltpu.SemaphoreType.DMA((1,))),
    )
    sums = across("gy", sums)
    (sums,) = call(total_kernel, "total", [(NX, LANES)], (sums,))
    sums = across("gx", sums)
    return tuple(call(update_kernel, "update", [direction.shape] * 3, (sums, image, live, iterate, residual, masked)))


def solution(mesh):
    points = P(None, "gx", "gy", None, None)
    blocks = P("gx", "gy", None)
    return jax.shard_map(
        on_device,
        mesh=mesh,
        in_specs=(points, points, points, points, points, blocks, blocks, blocks),
        out_specs=(points, points, points),
        check_vma=False,
    )
```

```python
import functools
import math

import jax
import jax.numpy as jnp
import ml_dtypes
import numpy as np
from jax import lax
from jax.experimental import pallas as pl
from jax.experimental.pallas import tpu as pltpu
from jax.sharding import PartitionSpec as P

G = 128
LENGTH = 2 * G
TL = 16
SPAN = 24
NX = 32
NY = 16
WIDE_ONE = G // NX
WIDE_TWO = G // NY
WIN_ONE = WIDE_ONE + 3
WIN_TWO = WIDE_TWO + 3
PAD_ONE = 8
PAD_TWO = 16
K_ONE = LENGTH // NX
K_TWO = LENGTH // NY
PARTS_X = 2 * WIN_ONE
ROWS_X = 10
EXTRA_X = PARTS_X - ROWS_X
HALF = PAD_TWO - WIN_TWO
ROWS_Y = 2 * WIN_TWO
LANES = 128
WIN_ROWS = 144
NOISE = 0.5
VMEM_LIMIT = 24 * 1024 * 1024
f32 = jnp.float32
bf16 = jnp.bfloat16


def rotation(out_index, in_index, sign, scale):
    turns = (np.outer(out_index, in_index) % LENGTH).astype(np.float64)
    angle = turns * (2.0 * math.pi / LENGTH)
    return np.cos(angle) * scale, sign * np.sin(angle) * scale


def table(out_index, out_ok, in_index, in_ok, sign, scale):
    parts = rotation(out_index, in_index, sign, scale)
    values = np.concatenate([np.where(out_ok[:, None] & in_ok[None, :], part, 0.0) for part in parts], axis=0)
    high = values.astype(ml_dtypes.bfloat16)
    low = (values - high.astype(np.float64)).astype(ml_dtypes.bfloat16)
    return np.concatenate([high, low, high], axis=1)


def window_index(owner, offset, wide):
    cell = owner * wide + offset - 1
    return cell, (cell >= 0) & (cell < G)


def cells_of(window, parity):
    return list(range(1 - parity, window, 2))


@functools.lru_cache(None)
def tables():
    def grid(*sizes):
        return [part.reshape(-1) for part in np.meshgrid(*[np.arange(size) for size in sizes], indexing="ij")]

    yes = lambda rows: np.ones(rows.shape, bool)
    n1 = np.arange(G)
    k1_low, k1_owner = grid(K_ONE, NX)
    k1 = k1_owner * K_ONE + k1_low
    first = table(k1, yes(k1), n1, yes(n1), -1.0, 1.0)
    first_back = table(n1, yes(n1), k1, yes(k1), 1.0, 1.0 / LENGTH)
    k2_low, k2_owner = grid(K_TWO, NY // 2)
    k2 = k2_owner * K_TWO + k2_low
    k3 = np.arange(LENGTH // 2)
    wholes = []
    for k, window, owners, wide in ((k2, WIN_ONE, NX, WIDE_ONE), (k3, WIN_TWO, NY, WIDE_TWO)):
        out, back = [], []
        for parity in range(2):
            cell, owner = grid(len(cells_of(window, parity)), owners)
            n, n_ok = window_index(owner, 2 * cell + 1 - parity, wide)
            out.append(table(k, yes(k), n, n_ok, -1.0, 1.0))
            back.append(table(n, n_ok, k, yes(k), 1.0, 1.0 / LENGTH))
        gap = np.zeros((out[1].shape[0], -out[1].shape[1] % LANES), ml_dtypes.bfloat16)
        wholes.append((np.concatenate([out[1], gap, out[0]], axis=1), np.concatenate(back, axis=0)))
    return first, wholes[0][0], wholes[1][0], wholes[1][1], wholes[0][1], first_back


def split(value):
    high = value.astype(bf16)
    return high, (value - high.astype(f32)).astype(bf16)


def dot(left, right, dims=((1,), (0,))):
    return lax.dot_general(left, right, (dims, ((), ())), preferred_element_type=f32)


def transform(table, real, imag):
    high, low = split(jnp.concatenate([real, imag], axis=1))
    data = jnp.concatenate([high, high, low], axis=0)
    rows = table.shape[0] // 2
    cos, sin = dot(table[:rows], data), dot(table[rows:], data)
    return cos[:, :LANES] - sin[:, LANES:], cos[:, LANES:] + sin[:, :LANES]


def transform_window(table_ref, parts, owners):
    results = []
    for parity in range(2):
        places = cells_of(len(parts[0]), parity)
        depth = 3 * len(places) * owners
        start = 0 if parity else table_ref.shape[1] - depth
        data = [jnp.concatenate([rows[place] for place in places], axis=0) for rows in parts]
        results.append(transform(table_ref[:, start : start + depth], *data))
    return [(even + odd, even - odd) for even, odd in zip(*results)]


def window_transform(table_ref, parts, window, owners):
    rows = [[None] * window for _ in parts]
    start = 0
    for parity in range(2):
        places = cells_of(window, parity)
        data = [low - high if parity else low + high for low, high in parts]
        end = start + 2 * len(places) * owners
        for part, columns in enumerate(transform(table_ref[start:end], *data)):
            for at, place in enumerate(places):
                rows[part][place] = columns[at * owners : (at + 1) * owners]
        start = end
    return rows


def exchange_turned(arrays, block, count):
    shape = arrays[0].shape
    place = lax.broadcasted_iota(jnp.int32, shape, 1) // block
    arrays = [pltpu.roll(array, index * block, 1) if index else array for index, array in enumerate(arrays)]
    arrays += [jnp.zeros(shape, f32)] * (count - len(arrays))
    step = 1
    while step < count:
        odd = (place // step) % 2 == 1
        arrays = [jnp.where(odd, arrays[(index + step) % count], arrays[index]) for index in range(count)]
        step *= 2
    return [
        pltpu.roll(arrays[count - index], LANES - index * block, 1) if index else arrays[0] for index in range(count)
    ]


def exchange(arrays, block):
    lane = lax.broadcasted_iota(jnp.int32, arrays[0].shape, 1)
    step = 1
    while step < len(arrays):
        width = step * block
        low = (lane // width) % 2 == 0
        mixed = list(arrays)
        for place in range(len(arrays)):
            if place & step:
                continue
            first, second = arrays[place], arrays[place | step]
            mixed[place] = jnp.where(low, first, pltpu.roll(second, width, 1))
            mixed[place | step] = jnp.where(low, pltpu.roll(first, LANES - width, 1), second)
        arrays = mixed
        step *= 2
    return arrays


def lane_cell(shape):
    return lax.broadcasted_iota(jnp.int32, shape, 1) % PAD_TWO


def pack(rows):
    cell = lane_cell(rows[0].shape)
    message = list(rows[:ROWS_X])
    for extra, row in enumerate(rows[ROWS_X:]):
        for half in range(2):
            moved = pltpu.roll(row, WIN_TWO - half * HALF, 1)
            place = 2 * extra + half
            message[place] = jnp.where(cell >= WIN_TWO, moved, message[place])
        place = 2 * EXTRA_X
        message[place] = jnp.where(cell == WIN_TWO + extra, pltpu.roll(row, 1 + extra, 1), message[place])
    return message


def unpack(message):
    cell = lane_cell(message[0].shape)
    rows = []
    for extra in range(EXTRA_X):
        row = pltpu.roll(message[2 * EXTRA_X], LANES - 1 - extra, 1)
        for half in (1, 0):
            moved = pltpu.roll(message[2 * extra + half], LANES - WIN_TWO + half * HALF, 1)
            row = jnp.where(cell < (half + 1) * HALF, moved, row)
        rows.append(row)
    return rows


def gather(ref, row, count, stride):
    return ref[pl.ds(row, count, stride=stride), :]


def live_slots(count_ref, shape):
    slot = lax.broadcasted_iota(jnp.int32, shape, 0)
    limit = jnp.zeros(shape, jnp.int32)
    for index in range(shape[0]):
        limit = jnp.where(slot == index, count_ref[0, 0, index], limit)
    return lax.broadcasted_iota(jnp.int32, shape, 1) < limit


def cubic_taps(fraction):
    frac_sq = fraction * fraction
    frac_cube = frac_sq * fraction
    return (
        -0.5 * frac_cube + frac_sq - 0.5 * fraction,
        1.5 * frac_cube - 2.5 * frac_sq + 1.0,
        -1.5 * frac_cube + 2.0 * frac_sq + 0.5 * fraction,
        0.5 * frac_cube - 0.5 * frac_sq,
    )


def stencil(first, taps, slot, extent):
    first_row = first[slot : slot + 1]
    offset = lax.broadcasted_iota(jnp.int32, (extent, first.shape[1]), 0) - first_row
    result = jnp.zeros(offset.shape, f32)
    for index in range(4):
        result = jnp.where(offset == index, taps[index][slot : slot + 1], result)
    return result


def point_weights(cells_ref, fracs_ref):
    firsts = [cells_ref[dim, 0, 0] & (wide - 1) for dim, wide in enumerate((TL, WIDE_ONE, WIDE_TWO))]
    taps = [cubic_taps(fracs_ref[dim, 0, 0]) for dim in range(3)]

    def weights(slot):
        depth = stencil(firsts[0], taps[0], slot, SPAN)
        across = stencil(firsts[1], taps[1], slot, PAD_ONE)
        upward = stencil(firsts[2], taps[2], slot, PAD_TWO)
        plane = across[:, None, :] * upward[None, :, :]
        return depth, plane.reshape(LANES, plane.shape[2])

    return weights


def spread_kernel(*refs):
    outside, refs = refs[:6], refs[6:]
    out_ref, masked_ref, live_ref, depth_ref, plane_ref, *inside, win_ref, sems = refs
    tile_ref, count_ref, dir_ref, cells_ref, fracs_ref, table_ref = inside
    copies = [pltpu.make_async_copy(far, near, sems.at[at]) for at, (far, near) in enumerate(zip(outside, inside))]
    for copy in copies:
        copy.start()
    win_ref[...] = jnp.zeros_like(win_ref)
    for copy in copies[:5]:
        copy.wait()
    probes, slots = dir_ref.shape[0], dir_ref.shape[3]
    live = live_slots(count_ref, dir_ref.shape[3:])
    live_ref[...] = live.astype(f32)
    masked = [jnp.where(live, dir_ref[probe, 0, 0], 0.0) for probe in range(probes)]
    for probe in range(probes):
        masked_ref[probe] = masked[probe]
    weights = point_weights(cells_ref, fracs_ref)
    for slot in range(slots):
        depth, plane = weights(slot)
        planes = jnp.concatenate(split(plane), axis=0)
        depth_ref[slot], plane_ref[slot] = depth, planes
        values = jnp.concatenate([depth * masked[probe][slot : slot + 1] for probe in range(probes)], axis=0)
        rows = values.shape[0]
        both = dot(jnp.concatenate(split(values), axis=0), planes, ((1,), (1,)))
        total = both[:rows, :LANES] + (both[:rows, LANES:] + both[rows:, :LANES])
        place = pl.ds(pl.multiple_of(tile_ref[0, 0, slot] * TL, TL), SPAN)
        for probe in range(probes):
            win_ref[probe, place, :] += total[probe * SPAN : (probe + 1) * SPAN]
    for copy in copies[5:]:
        copy.wait()
    rows = []
    for columns in transform(table_ref[...], win_ref[0, 1 : G + 1, :], win_ref[1, 1 : G + 1, :]):
        pieces = [columns[low * NX : (low + 1) * NX] for low in range(K_ONE)]
        rows += exchange(pieces, PAD_TWO)[:WIN_ONE]
    for row, piece in enumerate(pack(rows)):
        out_ref[pl.ds(row, NX, stride=ROWS_X), :] = piece


def window_rows(in_ref):
    rows = [gather(in_ref, row, NX, ROWS_X) for row in range(ROWS_X)]
    return rows + unpack(rows)


def second_kernel(in_ref, table_ref, out_ref):
    rows = window_rows(in_ref)
    parts = transform_window(table_ref, [rows[:WIN_ONE], rows[WIN_ONE:]], NX)
    half = NY // 2
    for part, halves in enumerate(parts):
        pieces = [
            jnp.concatenate([columns[low * half : (low + 1) * half] for columns in halves], axis=0)
            for low in range(K_TWO)
        ]
        for cell, piece in enumerate(exchange_turned(pieces, 1, PAD_TWO)[:WIN_TWO]):
            out_ref[pl.ds(2 * cell + part, NY, stride=ROWS_Y), :] = piece


def third_kernel(in_ref, spec_ref, table_ref, back_ref, out_ref):
    parts = [[gather(in_ref, 2 * cell + part, NY, ROWS_Y) for cell in range(WIN_TWO)] for part in range(2)]
    factor = spec_ref[...].reshape(LANES, LENGTH).T
    factors = factor[:G], factor[G:]
    scaled = [
        [columns * factor for columns, factor in zip(halves, factors)]
        for halves in transform_window(table_ref, parts, NY)
    ]
    for part, rows in enumerate(window_transform(back_ref, scaled, WIN_TWO, NY)):
        for cell, row in enumerate(rows):
            out_ref[pl.ds(2 * cell + part, NY, stride=ROWS_Y), :] = row


def fourth_kernel(in_ref, table_ref, out_ref):
    parts = []
    half = NY // 2
    for part in range(2):
        pieces = [gather(in_ref, 2 * cell + part, NY, ROWS_Y) for cell in range(WIN_TWO)]
        pieces = exchange_turned(pieces, 1, K_TWO)
        parts.append([jnp.concatenate([piece[at : at + half] for piece in pieces], axis=0) for at in (0, half)])
    rows = sum(window_transform(table_ref, parts, WIN_ONE, NX), [])
    for row, piece in enumerate(pack(rows)):
        out_ref[pl.ds(row, NX, stride=ROWS_X), :] = piece


def read_kernel(
    tile_far_ref, in_ref, res_ref, dir_ref, live_ref, depth_ref, plane_ref, table_ref,
    image_ref, sums_ref, tile_ref, win_ref, sems,
):
    copy = pltpu.make_async_copy(tile_far_ref, tile_ref, sems.at[0])
    copy.start()
    probes, slots = image_ref.shape[:2]
    rows = window_rows(in_ref)
    parts = []
    for part in range(2):
        pieces = rows[part * WIN_ONE : (part + 1) * WIN_ONE]
        parts.append(jnp.concatenate(exchange(pieces + [jnp.zeros((NX, LANES), f32)], PAD_TWO), axis=0))
    smooth = transform(table_ref[...], *parts)
    win_ref[...] = jnp.zeros_like(win_ref)
    for probe in range(probes):
        win_ref[probe, 1 : G + 1, :] = smooth[probe]
    copy.wait()
    for slot in range(slots):
        place = pl.ds(pl.multiple_of(tile_ref[0, 0, slot] * TL, TL), SPAN)
        block = jnp.concatenate([win_ref[probe, place, :] for probe in range(probes)], axis=0)
        block_high, block_low = split(block)
        rows = block.shape[0]
        left = jnp.concatenate([block_high, block_low], axis=0)
        right = jnp.concatenate([block_high, jnp.zeros_like(block_low)], axis=0)
        both = dot(jnp.concatenate([left, right], axis=1), plane_ref[slot])
        total = both[:rows] + both[rows:]
        for probe in range(probes):
            image_ref[probe, slot : slot + 1, :] = jnp.sum(
                depth_ref[slot] * total[probe * SPAN : (probe + 1) * SPAN], axis=0, keepdims=True
            )
    sums = []
    live = live_ref[...]
    for probe in range(probes):
        masked_res, masked_dir = live * res_ref[probe, 0, 0], dir_ref[probe]
        image = live * image_ref[probe] + NOISE * masked_dir
        image_ref[probe] = image
        for left, right in (
            (masked_res, masked_res),
            (masked_dir, image),
            (masked_res, image),
            (image, image),
        ):
            line = jnp.sum(left * right, axis=0, keepdims=True)
            sums.append(sum(line[:, at : at + LANES] for at in range(0, line.shape[1], LANES)))
    column = jnp.sum(jnp.concatenate(sums, axis=0), axis=1, keepdims=True)
    shape = (column.shape[0], LANES)
    own = lax.broadcasted_iota(jnp.int32, shape, 0) == lax.broadcasted_iota(jnp.int32, shape, 1)
    row = jnp.sum(jnp.where(own, column, 0.0), axis=0, keepdims=True)
    sums_ref[...] = jnp.broadcast_to(row, sums_ref.shape)


def total_kernel(in_ref, out_ref):
    out_ref[...] = jnp.broadcast_to(jnp.sum(in_ref[...], axis=0, keepdims=True), out_ref.shape)


def update_kernel(
    sums_ref, image_ref, live_ref, iterate_ref, res_ref, dir_ref, new_iterate_ref, new_res_ref, new_dir_ref
):
    sums = jnp.sum(sums_ref[...], axis=0, keepdims=True)
    live = live_ref[...]
    for probe in range(image_ref.shape[0]):
        old_norm, curvature, crossed, squared = (sums[:, 4 * probe + at : 4 * probe + at + 1] for at in range(4))
        alpha = old_norm / curvature
        new_norm = old_norm + alpha * (alpha * squared - 2.0 * crossed)
        beta = new_norm / old_norm
        masked_dir = dir_ref[probe]
        new_res = live * res_ref[probe, 0, 0] - alpha * image_ref[probe]
        new_iterate_ref[probe, 0, 0] = live * iterate_ref[probe, 0, 0] + alpha * masked_dir
        new_res_ref[probe, 0, 0] = new_res
        new_dir_ref[probe, 0, 0] = new_res + beta * masked_dir


def call(kernel, name, outs, operands, far=0, scratch=(), cost=None):
    operands = [pltpu.with_memory_space_constraint(operand, pltpu.HBM) for operand in operands[:far]] + [*operands[far:]]
    near = len(operands) - far
    outs = [jax.ShapeDtypeStruct(*(out if isinstance(out[0], tuple) else (out, f32))) for out in outs]
    return pl.pallas_call(
        kernel,
        out_shape=outs,
        in_specs=[pl.BlockSpec(memory_space=pltpu.HBM)] * far + [pl.BlockSpec(memory_space=pltpu.VMEM)] * near,
        out_specs=[pl.BlockSpec(memory_space=pltpu.VMEM)] * len(outs),
        scratch_shapes=list(scratch),
        compiler_params=pltpu.CompilerParams(vmem_limit_bytes=VMEM_LIMIT),
        cost_estimate=cost,
        name=name,
    )(*operands)


def across(axis, value):
    rows = value.shape[0]
    sent = value.reshape(rows, 1, LANES)
    return lax.all_to_all(sent, axis, split_axis=0, concat_axis=0, tiled=True).reshape(rows, LANES)


def on_device(iterate, residual, direction, cells, fracs, counts, slot_tile, spectrum):
    first, second, third, third_back, second_back, first_back = tables()
    probes, slots, cap = direction.shape[0], direction.shape[3], direction.shape[4]
    window = pltpu.VMEM((probes, WIN_ROWS, LANES), f32)
    operands = (slot_tile, counts, direction, cells, fracs, first)
    near = [
        (pltpu.SMEM if at < 2 else pltpu.VMEM)(operand.shape, operand.dtype) for at, operand in enumerate(operands)
    ]
    sent, masked, live, depth, planes = call(
        spread_kernel,
        "spread",
        [
            (NX * ROWS_X, LANES),
            (probes, slots, cap),
            (slots, cap),
            (slots, SPAN, cap),
            ((slots, 2 * LANES, cap), bf16),
        ],
        operands,
        far=len(operands),
        cost=pl.CostEstimate(flops=400_000_000, bytes_accessed=8_000_000, transcendentals=0),
        scratch=(*near, window, pltpu.SemaphoreType.DMA((len(operands),))),
    )
    came = across("gx", sent)
    (sent,) = call(second_kernel, "second", [(NY * ROWS_Y, LANES)], (came, second))
    came = across("gy", sent)
    (sent,) = call(third_kernel, "third", [(NY * ROWS_Y, LANES)], (came, spectrum, third, third_back))
    came = across("gy", sent)
    (sent,) = call(fourth_kernel, "fourth", [(NX * ROWS_X, LANES)], (came, second_back))
    came = across("gx", sent)
    image, sums = call(
        read_kernel,
        "read",
        [(probes, slots, cap), (NY, LANES)],
        (slot_tile, came, residual, masked, live, depth, planes, first_back),
        far=1,
        scratch=(near[0], window, pltpu.SemaphoreType.DMA((1,))),
    )
    sums = across("gy", sums)
    (sums,) = call(total_kernel, "total", [(NX, LANES)], (sums,))
    sums = across("gx", sums)
    return tuple(call(update_kernel, "update", [direction.shape] * 3, (sums, image, live, iterate, residual, masked)))


def solution(mesh):
    points = P(None, "gx", "gy", None, None)
    blocks = P("gx", "gy", None)
    return jax.shard_map(
        on_device,
        mesh=mesh,
        in_specs=(points, points, points, points, points, blocks, blocks, blocks),
        out_specs=(points, points, points),
        check_vma=False,
    )
```

```python
import functools
import math

import jax
import jax.numpy as jnp
import ml_dtypes
import numpy as np
from jax import lax
from jax.experimental import pallas as pl
from jax.experimental.pallas import tpu as pltpu
from jax.sharding import PartitionSpec as P

G = 128
LENGTH = 2 * G
TL = 16
SPAN = 24
NX = 32
NY = 16
WIDE_ONE = G // NX
WIDE_TWO = G // NY
WIN_ONE = WIDE_ONE + 3
WIN_TWO = WIDE_TWO + 3
PAD_ONE = 8
PAD_TWO = 16
K_ONE = LENGTH // NX
K_TWO = LENGTH // NY
PARTS_X = 2 * WIN_ONE
ROWS_X = 10
EXTRA_X = PARTS_X - ROWS_X
HALF = PAD_TWO - WIN_TWO
ROWS_Y = 2 * WIN_TWO
LANES = 128
WIN_ROWS = 144
NOISE = 0.5
VMEM_LIMIT = 24 * 1024 * 1024
f32 = jnp.float32
bf16 = jnp.bfloat16


def rotation(out_index, in_index, sign, scale):
    turns = (np.outer(out_index, in_index) % LENGTH).astype(np.float64)
    angle = turns * (2.0 * math.pi / LENGTH)
    return np.cos(angle) * scale, sign * np.sin(angle) * scale


def table(out_index, out_ok, in_index, in_ok, sign, scale):
    parts = rotation(out_index, in_index, sign, scale)
    values = np.concatenate([np.where(out_ok[:, None] & in_ok[None, :], part, 0.0) for part in parts], axis=0)
    high = values.astype(ml_dtypes.bfloat16)
    low = (values - high.astype(np.float64)).astype(ml_dtypes.bfloat16)
    return np.concatenate([high, low, high], axis=1)


def window_index(owner, offset, wide):
    cell = owner * wide + offset - 1
    return cell, (cell >= 0) & (cell < G)


def joined(even, odd):
    gap = np.zeros((odd.shape[0], -odd.shape[1] % LANES), ml_dtypes.bfloat16)
    return np.concatenate([odd, gap, even], axis=1)


def cells_of(window, parity):
    return list(range(1 - parity, window, 2))


@functools.lru_cache(None)
def tables():
    def grid(*sizes):
        return [part.reshape(-1) for part in np.meshgrid(*[np.arange(size) for size in sizes], indexing="ij")]

    yes = lambda rows: np.ones(rows.shape, bool)
    n1 = np.arange(G)
    k1_low, k1_owner = grid(K_ONE, NX)
    k1 = k1_owner * K_ONE + k1_low
    first_back = table(n1, yes(n1), k1, yes(k1), 1.0, 1.0 / LENGTH)
    k1_low, k1_owner = grid(K_ONE, NX // 2)
    k1 = k1_owner * K_ONE + k1_low
    first = joined(*[table(k1, yes(k1), n, yes(n), -1.0, 1.0) for n in (n1[0::2], n1[1::2])])
    k2_low, k2_owner = grid(K_TWO, NY // 2)
    k2 = k2_owner * K_TWO + k2_low
    k3 = np.arange(LENGTH // 2)
    wholes = []
    for k, window, owners, wide in ((k2, WIN_ONE, NX, WIDE_ONE), (k3, WIN_TWO, NY, WIDE_TWO)):
        out, back = [], []
        for parity in range(2):
            cell, owner = grid(len(cells_of(window, parity)), owners)
            n, n_ok = window_index(owner, 2 * cell + 1 - parity, wide)
            out.append(table(k, yes(k), n, n_ok, -1.0, 1.0))
            back.append(table(n, n_ok, k, yes(k), 1.0, 1.0 / LENGTH))
        wholes.append((joined(*out), np.concatenate(back, axis=0)))
    return first, wholes[0][0], wholes[1][0], wholes[1][1], wholes[0][1], first_back


def split(value):
    high = value.astype(bf16)
    return high, (value - high.astype(f32)).astype(bf16)


def dot(left, right, dims=((1,), (0,))):
    return lax.dot_general(left, right, (dims, ((), ())), preferred_element_type=f32)


def transform(table, real, imag):
    high, low = split(jnp.concatenate([real, imag], axis=1))
    data = jnp.concatenate([high, high, low], axis=0)
    rows = table.shape[0] // 2
    cos, sin = dot(table[:rows], data), dot(table[rows:], data)
    return cos[:, :LANES] - sin[:, LANES:], cos[:, LANES:] + sin[:, :LANES]


def transform_cells(table_ref, cells):
    results = []
    for parity, parts in enumerate(cells):
        depth = 3 * parts[0].shape[0]
        start = 0 if parity else table_ref.shape[1] - depth
        results.append(transform(table_ref[:, start : start + depth], *parts))
    return [(even + odd, even - odd) for even, odd in zip(*results)]


def transform_window(table_ref, parts):
    return transform_cells(
        table_ref,
        [
            [jnp.concatenate([rows[place] for place in cells_of(len(rows), parity)], axis=0) for rows in parts]
            for parity in range(2)
        ],
    )


def by_owner(halves, owners, count):
    half = owners // 2
    return [
        jnp.concatenate([columns[low * half : (low + 1) * half] for columns in halves], axis=0) for low in range(count)
    ]


def window_transform(table_ref, parts, window, owners):
    rows = [[None] * window for _ in parts]
    start = 0
    for parity in range(2):
        places = cells_of(window, parity)
        data = [low - high if parity else low + high for low, high in parts]
        end = start + 2 * len(places) * owners
        for part, columns in enumerate(transform(table_ref[start:end], *data)):
            for at, place in enumerate(places):
                rows[part][place] = columns[at * owners : (at + 1) * owners]
        start = end
    return rows


def exchange_turned(arrays, block, count):
    shape = arrays[0].shape
    place = lax.broadcasted_iota(jnp.int32, shape, 1) // block
    arrays = [pltpu.roll(array, index * block, 1) if index else array for index, array in enumerate(arrays)]
    arrays += [jnp.zeros(shape, f32)] * (count - len(arrays))
    step = 1
    while step < count:
        odd = (place // step) % 2 == 1
        arrays = [jnp.where(odd, arrays[(index + step) % count], arrays[index]) for index in range(count)]
        step *= 2
    return [
        pltpu.roll(arrays[count - index], LANES - index * block, 1) if index else arrays[0] for index in range(count)
    ]


def exchange(arrays, block):
    lane = lax.broadcasted_iota(jnp.int32, arrays[0].shape, 1)
    step = 1
    while step < len(arrays):
        width = step * block
        low = (lane // width) % 2 == 0
        mixed = list(arrays)
        for place in range(len(arrays)):
            if place & step:
                continue
            first, second = arrays[place], arrays[place | step]
            mixed[place] = jnp.where(low, first, pltpu.roll(second, width, 1))
            mixed[place | step] = jnp.where(low, pltpu.roll(first, LANES - width, 1), second)
        arrays = mixed
        step *= 2
    return arrays


def lane_cell(shape):
    return lax.broadcasted_iota(jnp.int32, shape, 1) % PAD_TWO


def pack(rows):
    cell = lane_cell(rows[0].shape)
    message = list(rows[:ROWS_X])
    for extra, row in enumerate(rows[ROWS_X:]):
        for half in range(2):
            moved = pltpu.roll(row, WIN_TWO - half * HALF, 1)
            place = 2 * extra + half
            message[place] = jnp.where(cell >= WIN_TWO, moved, message[place])
        place = 2 * EXTRA_X
        message[place] = jnp.where(cell == WIN_TWO + extra, pltpu.roll(row, 1 + extra, 1), message[place])
    return message


def unpack(message):
    cell = lane_cell(message[0].shape)
    rows = []
    for extra in range(EXTRA_X):
        row = pltpu.roll(message[2 * EXTRA_X], LANES - 1 - extra, 1)
        for half in (1, 0):
            moved = pltpu.roll(message[2 * extra + half], LANES - WIN_TWO + half * HALF, 1)
            row = jnp.where(cell < (half + 1) * HALF, moved, row)
        rows.append(row)
    return rows


def gather(ref, row, count, stride):
    return ref[pl.ds(row, count, stride=stride), :]


def live_slots(count_ref, shape):
    slot = lax.broadcasted_iota(jnp.int32, shape, 0)
    limit = jnp.zeros(shape, jnp.int32)
    for index in range(shape[0]):
        limit = jnp.where(slot == index, count_ref[0, 0, index], limit)
    return lax.broadcasted_iota(jnp.int32, shape, 1) < limit


def cubic_taps(fraction):
    frac_sq = fraction * fraction
    frac_cube = frac_sq * fraction
    return (
        -0.5 * frac_cube + frac_sq - 0.5 * fraction,
        1.5 * frac_cube - 2.5 * frac_sq + 1.0,
        -1.5 * frac_cube + 2.0 * frac_sq + 0.5 * fraction,
        0.5 * frac_cube - 0.5 * frac_sq,
    )


def stencil(first, taps, slot, extent):
    first_row = first[slot : slot + 1]
    offset = lax.broadcasted_iota(jnp.int32, (extent, first.shape[1]), 0) - first_row
    result = jnp.zeros(offset.shape, f32)
    for index in range(4):
        result = jnp.where(offset == index, taps[index][slot : slot + 1], result)
    return result


def point_weights(cells_ref, fracs_ref):
    firsts = [cells_ref[dim, 0, 0] & (wide - 1) for dim, wide in enumerate((TL, WIDE_ONE, WIDE_TWO))]
    taps = [cubic_taps(fracs_ref[dim, 0, 0]) for dim in range(3)]

    def weights(slot):
        depth = stencil(firsts[0], taps[0], slot, SPAN)
        across = stencil(firsts[1], taps[1], slot, PAD_ONE)
        upward = stencil(firsts[2], taps[2], slot, PAD_TWO)
        plane = across[:, None, :] * upward[None, :, :]
        return depth, plane.reshape(LANES, plane.shape[2])

    return weights


def spread_kernel(*refs):
    outside, refs = refs[:6], refs[6:]
    out_ref, masked_ref, live_ref, depth_ref, plane_ref, *inside, win_ref, sems = refs
    tile_ref, count_ref, dir_ref, cells_ref, fracs_ref, table_ref = inside
    copies = [pltpu.make_async_copy(far, near, sems.at[at]) for at, (far, near) in enumerate(zip(outside, inside))]
    for copy in copies:
        copy.start()
    win_ref[...] = jnp.zeros_like(win_ref)
    for copy in copies[:5]:
        copy.wait()
    probes, slots = dir_ref.shape[0], dir_ref.shape[3]
    live = live_slots(count_ref, dir_ref.shape[3:])
    live_ref[...] = live.astype(f32)
    masked = [jnp.where(live, dir_ref[probe, 0, 0], 0.0) for probe in range(probes)]
    for probe in range(probes):
        masked_ref[probe] = masked[probe]
    weights = point_weights(cells_ref, fracs_ref)
    for slot in range(slots):
        depth, plane = weights(slot)
        planes = jnp.concatenate(split(plane), axis=0)
        depth_ref[slot], plane_ref[slot] = depth, planes
        values = jnp.concatenate([depth * masked[probe][slot : slot + 1] for probe in range(probes)], axis=0)
        rows = values.shape[0]
        both = dot(jnp.concatenate(split(values), axis=0), planes, ((1,), (1,)))
        total = both[:rows, :LANES] + (both[:rows, LANES:] + both[rows:, :LANES])
        place = pl.ds(pl.multiple_of(tile_ref[0, 0, slot] * TL, TL), SPAN)
        for probe in range(probes):
            win_ref[probe, place, :] += total[probe * SPAN : (probe + 1) * SPAN]
    for copy in copies[5:]:
        copy.wait()
    cells = [[win_ref[probe, pl.ds(1 + parity, G // 2, stride=2), :] for probe in range(probes)] for parity in range(2)]
    rows = []
    for halves in transform_cells(table_ref, cells):
        pieces = by_owner(halves, NX, K_ONE)
        rows += exchange(pieces, PAD_TWO)[:WIN_ONE]
    for row, piece in enumerate(pack(rows)):
        out_ref[pl.ds(row, NX, stride=ROWS_X), :] = piece


def window_rows(in_ref):
    rows = [gather(in_ref, row, NX, ROWS_X) for row in range(ROWS_X)]
    return rows + unpack(rows)


def second_kernel(in_ref, table_ref, out_ref):
    rows = window_rows(in_ref)
    parts = transform_window(table_ref, [rows[:WIN_ONE], rows[WIN_ONE:]])
    for part, halves in enumerate(parts):
        pieces = by_owner(halves, NY, K_TWO)
        for cell, piece in enumerate(exchange_turned(pieces, 1, PAD_TWO)[:WIN_TWO]):
            out_ref[pl.ds(2 * cell + part, NY, stride=ROWS_Y), :] = piece


def third_kernel(in_ref, spec_ref, table_ref, back_ref, out_ref):
    parts = [[gather(in_ref, 2 * cell + part, NY, ROWS_Y) for cell in range(WIN_TWO)] for part in range(2)]
    factor = spec_ref[...].reshape(LANES, LENGTH).T
    factors = factor[:G], factor[G:]
    scaled = [
        [columns * factor for columns, factor in zip(halves, factors)]
        for halves in transform_window(table_ref, parts)
    ]
    for part, rows in enumerate(window_transform(back_ref, scaled, WIN_TWO, NY)):
        for cell, row in enumerate(rows):
            out_ref[pl.ds(2 * cell + part, NY, stride=ROWS_Y), :] = row


def fourth_kernel(in_ref, table_ref, out_ref):
    parts = []
    half = NY // 2
    for part in range(2):
        pieces = [gather(in_ref, 2 * cell + part, NY, ROWS_Y) for cell in range(WIN_TWO)]
        pieces = exchange_turned(pieces, 1, K_TWO)
        parts.append([jnp.concatenate([piece[at : at + half] for piece in pieces], axis=0) for at in (0, half)])
    rows = sum(window_transform(table_ref, parts, WIN_ONE, NX), [])
    for row, piece in enumerate(pack(rows)):
        out_ref[pl.ds(row, NX, stride=ROWS_X), :] = piece


def read_kernel(
    tile_far_ref, in_ref, res_ref, dir_ref, live_ref, depth_ref, plane_ref, table_ref,
    image_ref, sums_ref, tile_ref, win_ref, sems,
):
    copy = pltpu.make_async_copy(tile_far_ref, tile_ref, sems.at[0])
    copy.start()
    probes, slots = image_ref.shape[:2]
    rows = window_rows(in_ref)
    parts = []
    for part in range(2):
        pieces = rows[part * WIN_ONE : (part + 1) * WIN_ONE]
        parts.append(jnp.concatenate(exchange(pieces + [jnp.zeros((NX, LANES), f32)], PAD_TWO), axis=0))
    smooth = transform(table_ref[...], *parts)
    win_ref[...] = jnp.zeros_like(win_ref)
    for probe in range(probes):
        win_ref[probe, 1 : G + 1, :] = smooth[probe]
    copy.wait()
    for slot in range(slots):
        place = pl.ds(pl.multiple_of(tile_ref[0, 0, slot] * TL, TL), SPAN)
        block = jnp.concatenate([win_ref[probe, place, :] for probe in range(probes)], axis=0)
        block_high, block_low = split(block)
        rows = block.shape[0]
        left = jnp.concatenate([block_high, block_low], axis=0)
        right = jnp.concatenate([block_high, jnp.zeros_like(block_low)], axis=0)
        both = dot(jnp.concatenate([left, right], axis=1), plane_ref[slot])
        total = both[:rows] + both[rows:]
        for probe in range(probes):
            image_ref[probe, slot : slot + 1, :] = jnp.sum(
                depth_ref[slot] * total[probe * SPAN : (probe + 1) * SPAN], axis=0, keepdims=True
            )
    sums = []
    live = live_ref[...]
    for probe in range(probes):
        masked_res, masked_dir = live * res_ref[probe, 0, 0], dir_ref[probe]
        image = live * image_ref[probe] + NOISE * masked_dir
        image_ref[probe] = image
        for left, right in (
            (masked_res, masked_res),
            (masked_dir, image),
            (masked_res, image),
            (image, image),
        ):
            line = jnp.sum(left * right, axis=0, keepdims=True)
            sums.append(sum(line[:, at : at + LANES] for at in range(0, line.shape[1], LANES)))
    column = jnp.sum(jnp.concatenate(sums, axis=0), axis=1, keepdims=True)
    shape = (column.shape[0], LANES)
    own = lax.broadcasted_iota(jnp.int32, shape, 0) == lax.broadcasted_iota(jnp.int32, shape, 1)
    row = jnp.sum(jnp.where(own, column, 0.0), axis=0, keepdims=True)
    sums_ref[...] = jnp.broadcast_to(row, sums_ref.shape)


def total_kernel(in_ref, out_ref):
    out_ref[...] = jnp.broadcast_to(jnp.sum(in_ref[...], axis=0, keepdims=True), out_ref.shape)


def update_kernel(
    sums_ref, image_ref, live_ref, iterate_ref, res_ref, dir_ref, new_iterate_ref, new_res_ref, new_dir_ref
):
    sums = jnp.sum(sums_ref[...], axis=0, keepdims=True)
    live = live_ref[...]
    for probe in range(image_ref.shape[0]):
        old_norm, curvature, crossed, squared = (sums[:, 4 * probe + at : 4 * probe + at + 1] for at in range(4))
        alpha = old_norm / curvature
        new_norm = old_norm + alpha * (alpha * squared - 2.0 * crossed)
        beta = new_norm / old_norm
        masked_dir = dir_ref[probe]
        new_res = live * res_ref[probe, 0, 0] - alpha * image_ref[probe]
        new_iterate_ref[probe, 0, 0] = live * iterate_ref[probe, 0, 0] + alpha * masked_dir
        new_res_ref[probe, 0, 0] = new_res
        new_dir_ref[probe, 0, 0] = new_res + beta * masked_dir


def call(kernel, name, outs, operands, far=0, scratch=(), cost=None):
    operands = [pltpu.with_memory_space_constraint(operand, pltpu.HBM) for operand in operands[:far]] + [*operands[far:]]
    near = len(operands) - far
    outs = [jax.ShapeDtypeStruct(*(out if isinstance(out[0], tuple) else (out, f32))) for out in outs]
    return pl.pallas_call(
        kernel,
        out_shape=outs,
        in_specs=[pl.BlockSpec(memory_space=pltpu.HBM)] * far + [pl.BlockSpec(memory_space=pltpu.VMEM)] * near,
        out_specs=[pl.BlockSpec(memory_space=pltpu.VMEM)] * len(outs),
        scratch_shapes=list(scratch),
        compiler_params=pltpu.CompilerParams(vmem_limit_bytes=VMEM_LIMIT),
        cost_estimate=cost,
        name=name,
    )(*operands)


def across(axis, value):
    rows = value.shape[0]
    sent = value.reshape(rows, 1, LANES)
    return lax.all_to_all(sent, axis, split_axis=0, concat_axis=0, tiled=True).reshape(rows, LANES)


def on_device(iterate, residual, direction, cells, fracs, counts, slot_tile, spectrum):
    first, second, third, third_back, second_back, first_back = tables()
    probes, slots, cap = direction.shape[0], direction.shape[3], direction.shape[4]
    window = pltpu.VMEM((probes, WIN_ROWS, LANES), f32)
    operands = (slot_tile, counts, direction, cells, fracs, first)
    near = [
        (pltpu.SMEM if at < 2 else pltpu.VMEM)(operand.shape, operand.dtype) for at, operand in enumerate(operands)
    ]
    sent, masked, live, depth, planes = call(
        spread_kernel,
        "spread",
        [
            (NX * ROWS_X, LANES),
            (probes, slots, cap),
            (slots, cap),
            (slots, SPAN, cap),
            ((slots, 2 * LANES, cap), bf16),
        ],
        operands,
        far=len(operands),
        cost=pl.CostEstimate(flops=4_000_000_000, bytes_accessed=24_000_000, transcendentals=0),
        scratch=(*near, window, pltpu.SemaphoreType.DMA((len(operands),))),
    )
    came = across("gx", sent)
    (sent,) = call(second_kernel, "second", [(NY * ROWS_Y, LANES)], (came, second))
    came = across("gy", sent)
    (sent,) = call(third_kernel, "third", [(NY * ROWS_Y, LANES)], (came, spectrum, third, third_back))
    came = across("gy", sent)
    (sent,) = call(fourth_kernel, "fourth", [(NX * ROWS_X, LANES)], (came, second_back))
    came = across("gx", sent)
    image, sums = call(
        read_kernel,
        "read",
        [(probes, slots, cap), (NY, LANES)],
        (slot_tile, came, residual, masked, live, depth, planes, first_back),
        far=1,
        scratch=(near[0], window, pltpu.SemaphoreType.DMA((1,))),
    )
    sums = across("gy", sums)
    (sums,) = call(total_kernel, "total", [(NX, LANES)], (sums,))
    sums = across("gx", sums)
    return tuple(call(update_kernel, "update", [direction.shape] * 3, (sums, image, live, iterate, residual, masked)))


def solution(mesh):
    points = P(None, "gx", "gy", None, None)
    blocks = P("gx", "gy", None)
    return jax.shard_map(
        on_device,
        mesh=mesh,
        in_specs=(points, points, points, points, points, blocks, blocks, blocks),
        out_specs=(points, points, points),
        check_vma=False,
    )
```

```python
import functools
import math

import jax
import jax.numpy as jnp
import ml_dtypes
import numpy as np
from jax import lax
from jax.experimental import pallas as pl
from jax.experimental.pallas import tpu as pltpu
from jax.sharding import PartitionSpec as P

G = 128
LENGTH = 2 * G
TL = 16
SPAN = 24
NX = 32
NY = 16
WIDE_ONE = G // NX
WIDE_TWO = G // NY
WIN_ONE = WIDE_ONE + 3
WIN_TWO = WIDE_TWO + 3
PAD_ONE = 8
PAD_TWO = 16
K_ONE = LENGTH // NX
K_TWO = LENGTH // NY
PARTS_X = 2 * WIN_ONE
ROWS_X = 10
EXTRA_X = PARTS_X - ROWS_X
HALF = PAD_TWO - WIN_TWO
ROWS_Y = 2 * WIN_TWO
LANES = 128
WIN_ROWS = 144
NOISE = 0.5
VMEM_LIMIT = 24 * 1024 * 1024
f32 = jnp.float32
bf16 = jnp.bfloat16


def rotation(out_index, in_index, sign, scale):
    turns = (np.outer(out_index, in_index) % LENGTH).astype(np.float64)
    angle = turns * (2.0 * math.pi / LENGTH)
    return np.cos(angle) * scale, sign * np.sin(angle) * scale


def table(out_index, out_ok, in_index, in_ok, sign, scale):
    parts = rotation(out_index, in_index, sign, scale)
    values = np.concatenate([np.where(out_ok[:, None] & in_ok[None, :], part, 0.0) for part in parts], axis=0)
    high = values.astype(ml_dtypes.bfloat16)
    low = (values - high.astype(np.float64)).astype(ml_dtypes.bfloat16)
    return np.concatenate([high, low, high], axis=1)


def window_index(owner, offset, wide):
    cell = owner * wide + offset - 1
    return cell, (cell >= 0) & (cell < G)


def joined(even, odd):
    gap = np.zeros((odd.shape[0], -odd.shape[1] % LANES), ml_dtypes.bfloat16)
    return np.concatenate([odd, gap, even], axis=1)


def cells_of(window, parity):
    return list(range(1 - parity, window, 2))


@functools.lru_cache(None)
def tables():
    def grid(*sizes):
        return [part.reshape(-1) for part in np.meshgrid(*[np.arange(size) for size in sizes], indexing="ij")]

    yes = lambda rows: np.ones(rows.shape, bool)
    n1 = np.arange(G)
    k1_low, k1_owner = grid(K_ONE, NX)
    k1 = k1_owner * K_ONE + k1_low
    first_back = table(n1, yes(n1), k1, yes(k1), 1.0, 1.0 / LENGTH)
    k1_low, k1_owner = grid(K_ONE, NX // 2)
    k1 = k1_owner * K_ONE + k1_low
    first = joined(*[table(k1, yes(k1), n, yes(n), -1.0, 1.0) for n in (n1[0::2], n1[1::2])])
    k2_low, k2_owner = grid(K_TWO, NY // 2)
    k2 = k2_owner * K_TWO + k2_low
    k3 = np.arange(LENGTH // 2)
    wholes = []
    for k, window, owners, wide in ((k2, WIN_ONE, NX, WIDE_ONE), (k3, WIN_TWO, NY, WIDE_TWO)):
        out, back = [], []
        for parity in range(2):
            cell, owner = grid(len(cells_of(window, parity)), owners)
            n, n_ok = window_index(owner, 2 * cell + 1 - parity, wide)
            out.append(table(k, yes(k), n, n_ok, -1.0, 1.0))
            back.append(table(n, n_ok, k, yes(k), 1.0, 1.0 / LENGTH))
        wholes.append((joined(*out), np.concatenate(back, axis=0)))
    return first, wholes[0][0], wholes[1][0], wholes[1][1], wholes[0][1], first_back


def split(value):
    high = value.astype(bf16)
    return high, (value - high.astype(f32)).astype(bf16)


def dot(left, right, dims=((1,), (0,))):
    return lax.dot_general(left, right, (dims, ((), ())), preferred_element_type=f32)


def transform(table, real, imag):
    high, low = split(jnp.concatenate([real, imag], axis=1))
    data = jnp.concatenate([high, high, low], axis=0)
    rows = table.shape[0] // 2
    cos, sin = dot(table[:rows], data), dot(table[rows:], data)
    return cos[:, :LANES] - sin[:, LANES:], cos[:, LANES:] + sin[:, :LANES]


def transform_cells(table_ref, cells):
    results = []
    for parity, parts in enumerate(cells):
        depth = 3 * parts[0].shape[0]
        start = 0 if parity else table_ref.shape[1] - depth
        results.append(transform(table_ref[:, start : start + depth], *parts))
    return [(even + odd, even - odd) for even, odd in zip(*results)]


def transform_window(table_ref, parts):
    return transform_cells(
        table_ref,
        [
            [jnp.concatenate([rows[place] for place in cells_of(len(rows), parity)], axis=0) for rows in parts]
            for parity in range(2)
        ],
    )


def by_owner(halves, owners, count):
    half = owners // 2
    return [
        jnp.concatenate([columns[low * half : (low + 1) * half] for columns in halves], axis=0) for low in range(count)
    ]


def window_transform(table_ref, parts, window, owners):
    rows = [[None] * window for _ in parts]
    start = 0
    for parity in range(2):
        places = cells_of(window, parity)
        data = [low - high if parity else low + high for low, high in parts]
        end = start + 2 * len(places) * owners
        for part, columns in enumerate(transform(table_ref[start:end], *data)):
            for at, place in enumerate(places):
                rows[part][place] = columns[at * owners : (at + 1) * owners]
        start = end
    return rows


def exchange_turned(arrays, block, count):
    shape = arrays[0].shape
    place = lax.broadcasted_iota(jnp.int32, shape, 1) // block
    arrays = [pltpu.roll(array, index * block, 1) if index else array for index, array in enumerate(arrays)]
    arrays += [jnp.zeros(shape, f32)] * (count - len(arrays))
    step = 1
    while step < count:
        odd = (place // step) % 2 == 1
        arrays = [jnp.where(odd, arrays[(index + step) % count], arrays[index]) for index in range(count)]
        step *= 2
    return [
        pltpu.roll(arrays[count - index], LANES - index * block, 1) if index else arrays[0] for index in range(count)
    ]


def exchange(arrays, block):
    lane = lax.broadcasted_iota(jnp.int32, arrays[0].shape, 1)
    step = 1
    while step < len(arrays):
        width = step * block
        low = (lane // width) % 2 == 0
        mixed = list(arrays)
        for place in range(len(arrays)):
            if place & step:
                continue
            first, second = arrays[place], arrays[place | step]
            mixed[place] = jnp.where(low, first, pltpu.roll(second, width, 1))
            mixed[place | step] = jnp.where(low, pltpu.roll(first, LANES - width, 1), second)
        arrays = mixed
        step *= 2
    return arrays


def lane_cell(shape):
    return lax.broadcasted_iota(jnp.int32, shape, 1) % PAD_TWO


def pack(rows):
    cell = lane_cell(rows[0].shape)
    message = list(rows[:ROWS_X])
    for extra, row in enumerate(rows[ROWS_X:]):
        for half in range(2):
            moved = pltpu.roll(row, WIN_TWO - half * HALF, 1)
            place = 2 * extra + half
            message[place] = jnp.where(cell >= WIN_TWO, moved, message[place])
        place = 2 * EXTRA_X
        message[place] = jnp.where(cell == WIN_TWO + extra, pltpu.roll(row, 1 + extra, 1), message[place])
    return message


def unpack(message):
    cell = lane_cell(message[0].shape)
    rows = []
    for extra in range(EXTRA_X):
        row = pltpu.roll(message[2 * EXTRA_X], LANES - 1 - extra, 1)
        for half in (1, 0):
            moved = pltpu.roll(message[2 * extra + half], LANES - WIN_TWO + half * HALF, 1)
            row = jnp.where(cell < (half + 1) * HALF, moved, row)
        rows.append(row)
    return rows


def gather(ref, row, count, stride):
    return ref[pl.ds(row, count, stride=stride), :]


def live_slots(count_ref, shape):
    slot = lax.broadcasted_iota(jnp.int32, shape, 0)
    limit = jnp.zeros(shape, jnp.int32)
    for index in range(shape[0]):
        limit = jnp.where(slot == index, count_ref[0, 0, index], limit)
    return lax.broadcasted_iota(jnp.int32, shape, 1) < limit


def cubic_taps(fraction):
    frac_sq = fraction * fraction
    frac_cube = frac_sq * fraction
    return (
        -0.5 * frac_cube + frac_sq - 0.5 * fraction,
        1.5 * frac_cube - 2.5 * frac_sq + 1.0,
        -1.5 * frac_cube + 2.0 * frac_sq + 0.5 * fraction,
        0.5 * frac_cube - 0.5 * frac_sq,
    )


def stencil(first, taps, slot, extent):
    first_row = first[slot : slot + 1]
    offset = lax.broadcasted_iota(jnp.int32, (extent, first.shape[1]), 0) - first_row
    result = jnp.zeros(offset.shape, f32)
    for index in range(4):
        result = jnp.where(offset == index, taps[index][slot : slot + 1], result)
    return result


def point_weights(cells_ref, fracs_ref):
    firsts = [cells_ref[dim, 0, 0] & (wide - 1) for dim, wide in enumerate((TL, WIDE_ONE, WIDE_TWO))]
    taps = [cubic_taps(fracs_ref[dim, 0, 0]) for dim in range(3)]

    def weights(slot):
        depth = stencil(firsts[0], taps[0], slot, SPAN)
        across = stencil(firsts[1], taps[1], slot, PAD_ONE)
        upward = stencil(firsts[2], taps[2], slot, PAD_TWO)
        plane = across[:, None, :] * upward[None, :, :]
        return depth, plane.reshape(LANES, plane.shape[2])

    return weights


def spread_kernel(*refs):
    outside, refs = refs[:6], refs[6:]
    out_ref, masked_ref, live_ref, depth_ref, plane_ref, near_tile_ref, *inside, win_ref, sems = refs
    tile_ref, count_ref, dir_ref, cells_ref, fracs_ref, table_ref = inside
    copies = [pltpu.make_async_copy(far, near, sems.at[at]) for at, (far, near) in enumerate(zip(outside, inside))]
    copies.append(pltpu.make_async_copy(outside[0], near_tile_ref, sems.at[len(copies)]))
    for copy in copies:
        copy.start()
    win_ref[...] = jnp.zeros_like(win_ref)
    for copy in copies[:5]:
        copy.wait()
    probes, slots = dir_ref.shape[0], dir_ref.shape[3]
    live = live_slots(count_ref, dir_ref.shape[3:])
    live_ref[...] = live.astype(f32)
    masked = [jnp.where(live, dir_ref[probe, 0, 0], 0.0) for probe in range(probes)]
    for probe in range(probes):
        masked_ref[probe] = masked[probe]
    weights = point_weights(cells_ref, fracs_ref)
    for slot in range(slots):
        depth, plane = weights(slot)
        planes = jnp.concatenate(split(plane), axis=0)
        depth_ref[slot], plane_ref[slot] = depth, planes
        values = jnp.concatenate([depth * masked[probe][slot : slot + 1] for probe in range(probes)], axis=0)
        rows = values.shape[0]
        both = dot(jnp.concatenate(split(values), axis=0), planes, ((1,), (1,)))
        total = both[:rows, :LANES] + (both[:rows, LANES:] + both[rows:, :LANES])
        place = pl.ds(pl.multiple_of(tile_ref[0, 0, slot] * TL, TL), SPAN)
        for probe in range(probes):
            win_ref[probe, place, :] += total[probe * SPAN : (probe + 1) * SPAN]
    for copy in copies[5:]:
        copy.wait()
    cells = [[win_ref[probe, pl.ds(1 + parity, G // 2, stride=2), :] for probe in range(probes)] for parity in range(2)]
    rows = []
    for halves in transform_cells(table_ref, cells):
        pieces = by_owner(halves, NX, K_ONE)
        rows += exchange(pieces, PAD_TWO)[:WIN_ONE]
    for row, piece in enumerate(pack(rows)):
        out_ref[pl.ds(row, NX, stride=ROWS_X), :] = piece


def window_rows(in_ref):
    rows = [gather(in_ref, row, NX, ROWS_X) for row in range(ROWS_X)]
    return rows + unpack(rows)


def second_kernel(in_ref, table_ref, out_ref):
    rows = window_rows(in_ref)
    parts = transform_window(table_ref, [rows[:WIN_ONE], rows[WIN_ONE:]])
    for part, halves in enumerate(parts):
        pieces = by_owner(halves, NY, K_TWO)
        for cell, piece in enumerate(exchange_turned(pieces, 1, PAD_TWO)[:WIN_TWO]):
            out_ref[pl.ds(2 * cell + part, NY, stride=ROWS_Y), :] = piece


def third_kernel(in_ref, spec_ref, table_ref, back_ref, out_ref):
    parts = [[gather(in_ref, 2 * cell + part, NY, ROWS_Y) for cell in range(WIN_TWO)] for part in range(2)]
    factor = spec_ref[...].reshape(LANES, LENGTH).T
    factors = factor[:G], factor[G:]
    scaled = [
        [columns * factor for columns, factor in zip(halves, factors)]
        for halves in transform_window(table_ref, parts)
    ]
    for part, rows in enumerate(window_transform(back_ref, scaled, WIN_TWO, NY)):
        for cell, row in enumerate(rows):
            out_ref[pl.ds(2 * cell + part, NY, stride=ROWS_Y), :] = row


def fourth_kernel(in_ref, table_ref, out_ref):
    parts = []
    half = NY // 2
    for part in range(2):
        pieces = [gather(in_ref, 2 * cell + part, NY, ROWS_Y) for cell in range(WIN_TWO)]
        pieces = exchange_turned(pieces, 1, K_TWO)
        parts.append([jnp.concatenate([piece[at : at + half] for piece in pieces], axis=0) for at in (0, half)])
    rows = sum(window_transform(table_ref, parts, WIN_ONE, NX), [])
    for row, piece in enumerate(pack(rows)):
        out_ref[pl.ds(row, NX, stride=ROWS_X), :] = piece


def read_kernel(
    near_tile_ref, in_ref, res_ref, dir_ref, live_ref, depth_ref, plane_ref, table_ref,
    image_ref, sums_ref, win_ref,
):
    tile_row = near_tile_ref[0]
    own = lax.broadcasted_iota(jnp.int32, tile_row.shape, 1)
    tiles = [jnp.max(jnp.where(own == slot, tile_row, 0)) for slot in range(tile_row.shape[1])]
    probes, slots = image_ref.shape[:2]
    rows = window_rows(in_ref)
    parts = []
    for part in range(2):
        pieces = rows[part * WIN_ONE : (part + 1) * WIN_ONE]
        parts.append(jnp.concatenate(exchange_turned(pieces, PAD_TWO, K_ONE), axis=0))
    smooth = transform(table_ref[...], *parts)
    win_ref[...] = jnp.zeros_like(win_ref)
    for probe in range(probes):
        win_ref[probe, 1 : G + 1, :] = smooth[probe]
    for slot in range(slots):
        place = pl.ds(pl.multiple_of(tiles[slot] * TL, TL), SPAN)
        block = jnp.concatenate([win_ref[probe, place, :] for probe in range(probes)], axis=0)
        block_high, block_low = split(block)
        rows = block.shape[0]
        left = jnp.concatenate([block_high, block_low], axis=0)
        right = jnp.concatenate([block_high, jnp.zeros_like(block_low)], axis=0)
        both = dot(jnp.concatenate([left, right], axis=1), plane_ref[slot])
        total = both[:rows] + both[rows:]
        for probe in range(probes):
            image_ref[probe, slot : slot + 1, :] = jnp.sum(
                depth_ref[slot] * total[probe * SPAN : (probe + 1) * SPAN], axis=0, keepdims=True
            )
    sums = []
    live = live_ref[...]
    for probe in range(probes):
        masked_res, masked_dir = live * res_ref[probe, 0, 0], dir_ref[probe]
        image = live * image_ref[probe] + NOISE * masked_dir
        image_ref[probe] = image
        for left, right in (
            (masked_res, masked_res),
            (masked_dir, image),
            (masked_res, image),
            (image, image),
        ):
            line = jnp.sum(left * right, axis=0, keepdims=True)
            sums.append(sum(line[:, at : at + LANES] for at in range(0, line.shape[1], LANES)))
    column = jnp.sum(jnp.concatenate(sums, axis=0), axis=1, keepdims=True)
    shape = (column.shape[0], LANES)
    own = lax.broadcasted_iota(jnp.int32, shape, 0) == lax.broadcasted_iota(jnp.int32, shape, 1)
    row = jnp.sum(jnp.where(own, column, 0.0), axis=0, keepdims=True)
    sums_ref[...] = jnp.broadcast_to(row, sums_ref.shape)


def total_kernel(in_ref, out_ref):
    out_ref[...] = jnp.broadcast_to(jnp.sum(in_ref[...], axis=0, keepdims=True), out_ref.shape)


def update_kernel(
    sums_ref, image_ref, live_ref, iterate_ref, res_ref, dir_ref, new_iterate_ref, new_res_ref, new_dir_ref
):
    sums = jnp.sum(sums_ref[...], axis=0, keepdims=True)
    live = live_ref[...]
    for probe in range(image_ref.shape[0]):
        old_norm, curvature, crossed, squared = (sums[:, 4 * probe + at : 4 * probe + at + 1] for at in range(4))
        alpha = old_norm / curvature
        new_norm = old_norm + alpha * (alpha * squared - 2.0 * crossed)
        beta = new_norm / old_norm
        masked_dir = dir_ref[probe]
        new_res = live * res_ref[probe, 0, 0] - alpha * image_ref[probe]
        new_iterate_ref[probe, 0, 0] = live * iterate_ref[probe, 0, 0] + alpha * masked_dir
        new_res_ref[probe, 0, 0] = new_res
        new_dir_ref[probe, 0, 0] = new_res + beta * masked_dir


def call(kernel, name, outs, operands, far=0, scratch=(), cost=None):
    operands = [pltpu.with_memory_space_constraint(operand, pltpu.HBM) for operand in operands[:far]] + [*operands[far:]]
    near = len(operands) - far
    outs = [jax.ShapeDtypeStruct(*(out if isinstance(out[0], tuple) else (out, f32))) for out in outs]
    return pl.pallas_call(
        kernel,
        out_shape=outs,
        in_specs=[pl.BlockSpec(memory_space=pltpu.HBM)] * far + [pl.BlockSpec(memory_space=pltpu.VMEM)] * near,
        out_specs=[pl.BlockSpec(memory_space=pltpu.VMEM)] * len(outs),
        scratch_shapes=list(scratch),
        compiler_params=pltpu.CompilerParams(vmem_limit_bytes=VMEM_LIMIT),
        cost_estimate=cost,
        name=name,
    )(*operands)


def across(axis, value):
    rows = value.shape[0]
    sent = value.reshape(rows, 1, LANES)
    return lax.all_to_all(sent, axis, split_axis=0, concat_axis=0, tiled=True).reshape(rows, LANES)


def on_device(iterate, residual, direction, cells, fracs, counts, slot_tile, spectrum):
    first, second, third, third_back, second_back, first_back = tables()
    probes, slots, cap = direction.shape[0], direction.shape[3], direction.shape[4]
    window = pltpu.VMEM((probes, WIN_ROWS, LANES), f32)
    operands = (slot_tile, counts, direction, cells, fracs, first)
    near = [
        (pltpu.SMEM if at < 2 else pltpu.VMEM)(operand.shape, operand.dtype) for at, operand in enumerate(operands)
    ]
    sent, masked, live, depth, planes, near_tile = call(
        spread_kernel,
        "spread",
        [
            (NX * ROWS_X, LANES),
            (probes, slots, cap),
            (slots, cap),
            (slots, SPAN, cap),
            ((slots, 2 * LANES, cap), bf16),
            (slot_tile.shape, slot_tile.dtype),
        ],
        operands,
        far=len(operands),
        cost=pl.CostEstimate(flops=4_000_000_000, bytes_accessed=24_000_000, transcendentals=0),
        scratch=(*near, window, pltpu.SemaphoreType.DMA((len(operands) + 1,))),
    )
    came = across("gx", sent)
    (sent,) = call(second_kernel, "second", [(NY * ROWS_Y, LANES)], (came, second))
    came = across("gy", sent)
    (sent,) = call(third_kernel, "third", [(NY * ROWS_Y, LANES)], (came, spectrum, third, third_back))
    came = across("gy", sent)
    (sent,) = call(fourth_kernel, "fourth", [(NX * ROWS_X, LANES)], (came, second_back))
    came = across("gx", sent)
    image, sums = call(
        read_kernel,
        "read",
        [(probes, slots, cap), (NY, LANES)],
        (near_tile, came, residual, masked, live, depth, planes, first_back),
        scratch=(window,),
    )
    sums = across("gy", sums)
    (sums,) = call(total_kernel, "total", [(NX, LANES)], (sums,))
    sums = across("gx", sums)
    return tuple(call(update_kernel, "update", [direction.shape] * 3, (sums, image, live, iterate, residual, masked)))


def solution(mesh):
    points = P(None, "gx", "gy", None, None)
    blocks = P("gx", "gy", None)
    return jax.shard_map(
        on_device,
        mesh=mesh,
        in_specs=(points, points, points, points, points, blocks, blocks, blocks),
        out_specs=(points, points, points),
        check_vma=False,
    )
```

```python
import functools
import math

import jax
import jax.numpy as jnp
import ml_dtypes
import numpy as np
from jax import lax
from jax.experimental import pallas as pl
from jax.experimental.pallas import tpu as pltpu
from jax.sharding import PartitionSpec as P

G = 128
LENGTH = 2 * G
TL = 16
SPAN = 24
NX = 32
NY = 16
WIDE_ONE = G // NX
WIDE_TWO = G // NY
WIN_ONE = WIDE_ONE + 3
WIN_TWO = WIDE_TWO + 3
PAD_ONE = 8
PAD_TWO = 16
K_ONE = LENGTH // NX
K_TWO = LENGTH // NY
PARTS_X = 2 * WIN_ONE
ROWS_X = 10
EXTRA_X = PARTS_X - ROWS_X
HALF = PAD_TWO - WIN_TWO
ROWS_Y = 2 * WIN_TWO
LANES = 128
WIN_ROWS = 144
NOISE = 0.5
VMEM_LIMIT = 24 * 1024 * 1024
f32 = jnp.float32
bf16 = jnp.bfloat16


def rotation(out_index, in_index, sign, scale):
    turns = (np.outer(out_index, in_index) % LENGTH).astype(np.float64)
    angle = turns * (2.0 * math.pi / LENGTH)
    return np.cos(angle) * scale, sign * np.sin(angle) * scale


def table(out_index, out_ok, in_index, in_ok, sign, scale):
    parts = rotation(out_index, in_index, sign, scale)
    values = np.concatenate([np.where(out_ok[:, None] & in_ok[None, :], part, 0.0) for part in parts], axis=0)
    high = values.astype(ml_dtypes.bfloat16)
    low = (values - high.astype(np.float64)).astype(ml_dtypes.bfloat16)
    return np.concatenate([high, low, high], axis=1)


def window_index(owner, offset, wide):
    cell = owner * wide + offset - 1
    return cell, (cell >= 0) & (cell < G)


def joined(even, odd):
    gap = np.zeros((odd.shape[0], -odd.shape[1] % LANES), ml_dtypes.bfloat16)
    return np.concatenate([odd, gap, even], axis=1)


def cells_of(window, parity):
    return list(range(1 - parity, window, 2))


@functools.lru_cache(None)
def tables():
    def grid(*sizes):
        return [part.reshape(-1) for part in np.meshgrid(*[np.arange(size) for size in sizes], indexing="ij")]

    yes = lambda rows: np.ones(rows.shape, bool)
    n1 = np.arange(G)
    k1_low, k1_owner = grid(K_ONE, NX)
    k1 = k1_owner * K_ONE + k1_low
    first_back = table(n1, yes(n1), k1, yes(k1), 1.0, 1.0 / LENGTH)
    k1_low, k1_owner = grid(K_ONE, NX // 2)
    k1 = k1_owner * K_ONE + k1_low
    first = joined(*[table(k1, yes(k1), n, yes(n), -1.0, 1.0) for n in (n1[0::2], n1[1::2])])
    k2_low, k2_owner = grid(K_TWO, NY // 2)
    k2 = k2_owner * K_TWO + k2_low
    k3 = np.arange(LENGTH // 2)
    wholes = []
    for k, window, owners, wide in ((k2, WIN_ONE, NX, WIDE_ONE), (k3, WIN_TWO, NY, WIDE_TWO)):
        out, back = [], []
        for parity in range(2):
            cell, owner = grid(len(cells_of(window, parity)), owners)
            n, n_ok = window_index(owner, 2 * cell + 1 - parity, wide)
            out.append(table(k, yes(k), n, n_ok, -1.0, 1.0))
            back.append(table(n, n_ok, k, yes(k), 1.0, 1.0 / LENGTH))
        wholes.append((joined(*out), np.concatenate(back, axis=0)))
    return first, wholes[0][0], wholes[1][0], wholes[1][1], wholes[0][1], first_back


def split(value):
    high = value.astype(bf16)
    return high, (value - high.astype(f32)).astype(bf16)


def dot(left, right, dims=((1,), (0,))):
    return lax.dot_general(left, right, (dims, ((), ())), preferred_element_type=f32)


def transform(table, real, imag):
    high, low = split(jnp.concatenate([real, imag], axis=1))
    data = jnp.concatenate([high, high, low], axis=0)
    rows = table.shape[0] // 2
    cos, sin = dot(table[:rows], data), dot(table[rows:], data)
    return cos[:, :LANES] - sin[:, LANES:], cos[:, LANES:] + sin[:, :LANES]


def transform_cells(table_ref, cells):
    results = []
    for parity, parts in enumerate(cells):
        depth = 3 * parts[0].shape[0]
        start = 0 if parity else table_ref.shape[1] - depth
        results.append(transform(table_ref[:, start : start + depth], *parts))
    return [(even + odd, even - odd) for even, odd in zip(*results)]


def transform_window(table_ref, parts):
    return transform_cells(
        table_ref,
        [
            [jnp.concatenate([rows[place] for place in cells_of(len(rows), parity)], axis=0) for rows in parts]
            for parity in range(2)
        ],
    )


def by_owner(halves, owners, count):
    half = owners // 2
    return [
        jnp.concatenate([columns[low * half : (low + 1) * half] for columns in halves], axis=0) for low in range(count)
    ]


def window_transform(table_ref, parts, window, owners):
    rows = [[None] * window for _ in parts]
    start = 0
    for parity in range(2):
        places = cells_of(window, parity)
        data = [low - high if parity else low + high for low, high in parts]
        end = start + 2 * len(places) * owners
        for part, columns in enumerate(transform(table_ref[start:end], *data)):
            for at, place in enumerate(places):
                rows[part][place] = columns[at * owners : (at + 1) * owners]
        start = end
    return rows


def exchange_turned(arrays, block, count):
    shape = arrays[0].shape
    place = lax.broadcasted_iota(jnp.int32, shape, 1) // block
    arrays = [pltpu.roll(array, index * block, 1) if index else array for index, array in enumerate(arrays)]
    arrays += [jnp.zeros(shape, f32)] * (count - len(arrays))
    step = 1
    while step < count:
        odd = (place // step) % 2 == 1
        arrays = [jnp.where(odd, arrays[(index + step) % count], arrays[index]) for index in range(count)]
        step *= 2
    return [
        pltpu.roll(arrays[count - index], LANES - index * block, 1) if index else arrays[0] for index in range(count)
    ]


def exchange(arrays, block):
    lane = lax.broadcasted_iota(jnp.int32, arrays[0].shape, 1)
    step = 1
    while step < len(arrays):
        width = step * block
        low = (lane // width) % 2 == 0
        mixed = list(arrays)
        for place in range(len(arrays)):
            if place & step:
                continue
            first, second = arrays[place], arrays[place | step]
            mixed[place] = jnp.where(low, first, pltpu.roll(second, width, 1))
            mixed[place | step] = jnp.where(low, pltpu.roll(first, LANES - width, 1), second)
        arrays = mixed
        step *= 2
    return arrays


def lane_cell(shape):
    return lax.broadcasted_iota(jnp.int32, shape, 1) % PAD_TWO


def pack(rows):
    cell = lane_cell(rows[0].shape)
    message = list(rows[:ROWS_X])
    for extra, row in enumerate(rows[ROWS_X:]):
        for half in range(2):
            moved = pltpu.roll(row, WIN_TWO - half * HALF, 1)
            place = 2 * extra + half
            message[place] = jnp.where(cell >= WIN_TWO, moved, message[place])
        place = 2 * EXTRA_X
        message[place] = jnp.where(cell == WIN_TWO + extra, pltpu.roll(row, 1 + extra, 1), message[place])
    return message


def unpack(message):
    cell = lane_cell(message[0].shape)
    rows = []
    for extra in range(EXTRA_X):
        row = pltpu.roll(message[2 * EXTRA_X], LANES - 1 - extra, 1)
        for half in (1, 0):
            moved = pltpu.roll(message[2 * extra + half], LANES - WIN_TWO + half * HALF, 1)
            row = jnp.where(cell < (half + 1) * HALF, moved, row)
        rows.append(row)
    return rows


def gather(ref, row, count, stride):
    return ref[pl.ds(row, count, stride=stride), :]


def live_slots(count_ref, shape):
    slot = lax.broadcasted_iota(jnp.int32, shape, 0)
    limit = jnp.zeros(shape, jnp.int32)
    for index in range(shape[0]):
        limit = jnp.where(slot == index, count_ref[0, 0, index], limit)
    return lax.broadcasted_iota(jnp.int32, shape, 1) < limit


def cubic_taps(fraction):
    frac_sq = fraction * fraction
    frac_cube = frac_sq * fraction
    return (
        -0.5 * frac_cube + frac_sq - 0.5 * fraction,
        1.5 * frac_cube - 2.5 * frac_sq + 1.0,
        -1.5 * frac_cube + 2.0 * frac_sq + 0.5 * fraction,
        0.5 * frac_cube - 0.5 * frac_sq,
    )


def stencil(first, taps, slot, extent):
    first_row = first[slot : slot + 1]
    offset = lax.broadcasted_iota(jnp.int32, (extent, first.shape[1]), 0) - first_row
    result = jnp.zeros(offset.shape, f32)
    for index in range(4):
        result = jnp.where(offset == index, taps[index][slot : slot + 1], result)
    return result


def point_weights(cells_ref, fracs_ref):
    firsts = [cells_ref[dim, 0, 0] & (wide - 1) for dim, wide in enumerate((TL, WIDE_ONE, WIDE_TWO))]
    taps = [cubic_taps(fracs_ref[dim, 0, 0]) for dim in range(3)]

    def weights(slot):
        depth = stencil(firsts[0], taps[0], slot, SPAN)
        across = stencil(firsts[1], taps[1], slot, PAD_ONE)
        upward = stencil(firsts[2], taps[2], slot, PAD_TWO)
        plane = across[:, None, :] * upward[None, :, :]
        return depth, plane.reshape(LANES, plane.shape[2])

    return weights


def spread_kernel(*refs):
    outside, refs = refs[:6], refs[6:]
    out_ref, masked_ref, live_ref, depth_ref, plane_ref, near_tile_ref, *inside, win_ref, sems = refs
    tile_ref, count_ref, dir_ref, cells_ref, fracs_ref, table_ref = inside
    copies = [pltpu.make_async_copy(far, near, sems.at[at]) for at, (far, near) in enumerate(zip(outside, inside))]
    copies.append(pltpu.make_async_copy(outside[0], near_tile_ref, sems.at[len(copies)]))
    for copy in copies:
        copy.start()
    win_ref[...] = jnp.zeros_like(win_ref)
    for copy in copies[:5]:
        copy.wait()
    probes, slots = dir_ref.shape[0], dir_ref.shape[3]
    live = live_slots(count_ref, dir_ref.shape[3:])
    live_ref[...] = live.astype(f32)
    masked = [jnp.where(live, dir_ref[probe, 0, 0], 0.0) for probe in range(probes)]
    for probe in range(probes):
        masked_ref[probe] = masked[probe]
    weights = point_weights(cells_ref, fracs_ref)
    for slot in range(slots):
        depth, plane = weights(slot)
        planes = jnp.concatenate(split(plane), axis=0)
        depth_ref[slot], plane_ref[slot] = depth, planes
        values = jnp.concatenate([depth * masked[probe][slot : slot + 1] for probe in range(probes)], axis=0)
        rows = values.shape[0]
        both = dot(jnp.concatenate(split(values), axis=0), planes, ((1,), (1,)))
        total = both[:rows, :LANES] + (both[:rows, LANES:] + both[rows:, :LANES])
        place = pl.ds(pl.multiple_of(tile_ref[0, 0, slot] * TL, TL), SPAN)
        for probe in range(probes):
            win_ref[probe, place, :] += total[probe * SPAN : (probe + 1) * SPAN]
    for copy in copies[5:]:
        copy.wait()
    cells = [[win_ref[probe, pl.ds(1 + parity, G // 2, stride=2), :] for probe in range(probes)] for parity in range(2)]
    rows = []
    for halves in transform_cells(table_ref, cells):
        pieces = by_owner(halves, NX, K_ONE)
        rows += exchange(pieces, PAD_TWO)[:WIN_ONE]
    for row, piece in enumerate(pack(rows)):
        out_ref[pl.ds(row, NX, stride=ROWS_X), :] = piece


def window_rows(in_ref):
    rows = [gather(in_ref, row, NX, ROWS_X) for row in range(ROWS_X)]
    return rows + unpack(rows)


def second_kernel(in_ref, table_ref, out_ref):
    rows = window_rows(in_ref)
    parts = transform_window(table_ref, [rows[:WIN_ONE], rows[WIN_ONE:]])
    for part, halves in enumerate(parts):
        pieces = by_owner(halves, NY, K_TWO)
        for cell, piece in enumerate(exchange_turned(pieces, 1, PAD_TWO)[:WIN_TWO]):
            out_ref[pl.ds(2 * cell + part, NY, stride=ROWS_Y), :] = piece


def third_kernel(in_ref, spec_ref, table_ref, back_ref, out_ref):
    parts = [[gather(in_ref, 2 * cell + part, NY, ROWS_Y) for cell in range(WIN_TWO)] for part in range(2)]
    factor = spec_ref[...].reshape(LANES, LENGTH).T
    factors = factor[:G], factor[G:]
    scaled = [
        [columns * factor for columns, factor in zip(halves, factors)]
        for halves in transform_window(table_ref, parts)
    ]
    for part, rows in enumerate(window_transform(back_ref, scaled, WIN_TWO, NY)):
        for cell, row in enumerate(rows):
            out_ref[pl.ds(2 * cell + part, NY, stride=ROWS_Y), :] = row


def fourth_kernel(in_ref, table_ref, out_ref):
    parts = []
    half = NY // 2
    for part in range(2):
        pieces = [gather(in_ref, 2 * cell + part, NY, ROWS_Y) for cell in range(WIN_TWO)]
        pieces = exchange_turned(pieces, 1, K_TWO)
        parts.append([jnp.concatenate([piece[at : at + half] for piece in pieces], axis=0) for at in (0, half)])
    rows = sum(window_transform(table_ref, parts, WIN_ONE, NX), [])
    for row, piece in enumerate(pack(rows)):
        out_ref[pl.ds(row, NX, stride=ROWS_X), :] = piece


def read_kernel(
    near_tile_ref, in_ref, res_ref, dir_ref, live_ref, depth_ref, plane_ref, table_ref,
    image_ref, sums_ref, win_ref,
):
    tile_row = near_tile_ref[0]
    own = lax.broadcasted_iota(jnp.int32, tile_row.shape, 1)
    tiles = [jnp.max(jnp.where(own == slot, tile_row, 0)) for slot in range(tile_row.shape[1])]
    probes, slots = image_ref.shape[:2]
    rows = window_rows(in_ref)
    parts = []
    for part in range(2):
        pieces = rows[part * WIN_ONE : (part + 1) * WIN_ONE]
        parts.append(jnp.concatenate(exchange_turned(pieces, PAD_TWO, K_ONE), axis=0))
    smooth = transform(table_ref[...], *parts)
    win_ref[...] = jnp.zeros_like(win_ref)
    for probe in range(probes):
        win_ref[probe, 1 : G + 1, :] = smooth[probe]
    for slot in range(slots):
        place = pl.ds(pl.multiple_of(tiles[slot] * TL, TL), SPAN)
        block = jnp.concatenate([win_ref[probe, place, :] for probe in range(probes)], axis=0)
        block_high, block_low = split(block)
        rows = block.shape[0]
        left = jnp.concatenate([block_high, block_low], axis=0)
        right = jnp.concatenate([block_high, jnp.zeros_like(block_low)], axis=0)
        both = dot(jnp.concatenate([left, right], axis=1), plane_ref[slot])
        total = both[:rows] + both[rows:]
        for probe in range(probes):
            image_ref[probe, slot : slot + 1, :] = jnp.sum(
                depth_ref[slot] * total[probe * SPAN : (probe + 1) * SPAN], axis=0, keepdims=True
            )
    sums = []
    live = live_ref[...]
    for probe in range(probes):
        masked_res, masked_dir = live * res_ref[probe, 0, 0], dir_ref[probe]
        image = live * image_ref[probe] + NOISE * masked_dir
        image_ref[probe] = image
        for left, right in (
            (masked_res, masked_res),
            (masked_dir, image),
            (masked_res, image),
            (image, image),
        ):
            line = jnp.sum(left * right, axis=0, keepdims=True)
            sums.append(sum(line[:, at : at + LANES] for at in range(0, line.shape[1], LANES)))
    column = jnp.sum(jnp.concatenate(sums, axis=0), axis=1, keepdims=True)
    shape = (column.shape[0], LANES)
    own = lax.broadcasted_iota(jnp.int32, shape, 0) == lax.broadcasted_iota(jnp.int32, shape, 1)
    row = jnp.sum(jnp.where(own, column, 0.0), axis=0, keepdims=True)
    sums_ref[...] = jnp.broadcast_to(row, sums_ref.shape)


def update_kernel(
    sums_ref, image_ref, live_ref, iterate_ref, res_ref, dir_ref, new_iterate_ref, new_res_ref, new_dir_ref
):
    sums = jnp.sum(sums_ref[...], axis=0, keepdims=True)
    live = live_ref[...]
    for probe in range(image_ref.shape[0]):
        old_norm, curvature, crossed, squared = (sums[:, 4 * probe + at : 4 * probe + at + 1] for at in range(4))
        alpha = old_norm / curvature
        new_norm = old_norm + alpha * (alpha * squared - 2.0 * crossed)
        beta = new_norm / old_norm
        masked_dir = dir_ref[probe]
        new_res = live * res_ref[probe, 0, 0] - alpha * image_ref[probe]
        new_iterate_ref[probe, 0, 0] = live * iterate_ref[probe, 0, 0] + alpha * masked_dir
        new_res_ref[probe, 0, 0] = new_res
        new_dir_ref[probe, 0, 0] = new_res + beta * masked_dir


def call(kernel, name, outs, operands, far=0, scratch=(), cost=None):
    operands = [pltpu.with_memory_space_constraint(operand, pltpu.HBM) for operand in operands[:far]] + [*operands[far:]]
    near = len(operands) - far
    outs = [jax.ShapeDtypeStruct(*(out if isinstance(out[0], tuple) else (out, f32))) for out in outs]
    return pl.pallas_call(
        kernel,
        out_shape=outs,
        in_specs=[pl.BlockSpec(memory_space=pltpu.HBM)] * far + [pl.BlockSpec(memory_space=pltpu.VMEM)] * near,
        out_specs=[pl.BlockSpec(memory_space=pltpu.VMEM)] * len(outs),
        scratch_shapes=list(scratch),
        compiler_params=pltpu.CompilerParams(vmem_limit_bytes=VMEM_LIMIT),
        cost_estimate=cost,
        name=name,
    )(*operands)


def across(axis, value):
    rows = value.shape[0]
    sent = value.reshape(rows, 1, LANES)
    return lax.all_to_all(sent, axis, split_axis=0, concat_axis=0, tiled=True).reshape(rows, LANES)


def on_device(iterate, residual, direction, cells, fracs, counts, slot_tile, spectrum):
    first, second, third, third_back, second_back, first_back = tables()
    probes, slots, cap = direction.shape[0], direction.shape[3], direction.shape[4]
    window = pltpu.VMEM((probes, WIN_ROWS, LANES), f32)
    operands = (slot_tile, counts, direction, cells, fracs, first)
    near = [
        (pltpu.SMEM if at < 2 else pltpu.VMEM)(operand.shape, operand.dtype) for at, operand in enumerate(operands)
    ]
    sent, masked, live, depth, planes, near_tile = call(
        spread_kernel,
        "spread",
        [
            (NX * ROWS_X, LANES),
            (probes, slots, cap),
            (slots, cap),
            (slots, SPAN, cap),
            ((slots, 2 * LANES, cap), bf16),
            (slot_tile.shape, slot_tile.dtype),
        ],
        operands,
        far=len(operands),
        cost=pl.CostEstimate(flops=4_000_000_000, bytes_accessed=24_000_000, transcendentals=0),
        scratch=(*near, window, pltpu.SemaphoreType.DMA((len(operands) + 1,))),
    )
    came = across("gx", sent)
    (sent,) = call(second_kernel, "second", [(NY * ROWS_Y, LANES)], (came, second))
    came = across("gy", sent)
    (sent,) = call(third_kernel, "third", [(NY * ROWS_Y, LANES)], (came, spectrum, third, third_back))
    came = across("gy", sent)
    (sent,) = call(fourth_kernel, "fourth", [(NX * ROWS_X, LANES)], (came, second_back))
    came = across("gx", sent)
    image, sums = call(
        read_kernel,
        "read",
        [(probes, slots, cap), (NX * NY, LANES)],
        (near_tile, came, residual, masked, live, depth, planes, first_back),
        scratch=(window,),
    )
    sums = across(("gx", "gy"), sums)
    return tuple(call(update_kernel, "update", [direction.shape] * 3, (sums, image, live, iterate, residual, masked)))


def solution(mesh):
    points = P(None, "gx", "gy", None, None)
    blocks = P("gx", "gy", None)
    return jax.shard_map(
        on_device,
        mesh=mesh,
        in_specs=(points, points, points, points, points, blocks, blocks, blocks),
        out_specs=(points, points, points),
        check_vma=False,
    )
```

```python
import functools
import math

import jax
import jax.numpy as jnp
import ml_dtypes
import numpy as np
from jax import lax
from jax.experimental import pallas as pl
from jax.experimental.pallas import tpu as pltpu
from jax.sharding import PartitionSpec as P

G = 128
LENGTH = 2 * G
TL = 16
SPAN = 24
NX = 32
NY = 16
WIDE_ONE = G // NX
WIDE_TWO = G // NY
WIN_ONE = WIDE_ONE + 3
WIN_TWO = WIDE_TWO + 3
PAD_ONE = 8
PAD_TWO = 16
K_ONE = LENGTH // NX
K_TWO = LENGTH // NY
PARTS_X = 2 * WIN_ONE
ROWS_X = 10
EXTRA_X = PARTS_X - ROWS_X
HALF = PAD_TWO - WIN_TWO
ROWS_Y = 2 * WIN_TWO
LANES = 128
WIN_ROWS = 144
NOISE = 0.5
VMEM_LIMIT = 24 * 1024 * 1024
f32 = jnp.float32
bf16 = jnp.bfloat16


def rotation(out_index, in_index, sign, scale):
    turns = (np.outer(out_index, in_index) % LENGTH).astype(np.float64)
    angle = turns * (2.0 * math.pi / LENGTH)
    return np.cos(angle) * scale, sign * np.sin(angle) * scale


def table(out_index, out_ok, in_index, in_ok, sign, scale):
    parts = rotation(out_index, in_index, sign, scale)
    values = np.concatenate([np.where(out_ok[:, None] & in_ok[None, :], part, 0.0) for part in parts], axis=0)
    high = values.astype(ml_dtypes.bfloat16)
    low = (values - high.astype(np.float64)).astype(ml_dtypes.bfloat16)
    return np.concatenate([high, low, high], axis=1)


def window_index(owner, offset, wide):
    cell = owner * wide + offset - 1
    return cell, (cell >= 0) & (cell < G)


def joined(even, odd):
    gap = np.zeros((odd.shape[0], -odd.shape[1] % LANES), ml_dtypes.bfloat16)
    return np.concatenate([odd, gap, even], axis=1)


def cells_of(window, parity):
    return list(range(1 - parity, window, 2))


@functools.lru_cache(None)
def tables():
    def grid(*sizes):
        return [part.reshape(-1) for part in np.meshgrid(*[np.arange(size) for size in sizes], indexing="ij")]

    yes = lambda rows: np.ones(rows.shape, bool)
    n1 = np.arange(G)
    k1_low, k1_owner = grid(K_ONE, NX)
    k1 = k1_owner * K_ONE + k1_low
    first_back = table(n1, yes(n1), k1, yes(k1), 1.0, 1.0 / LENGTH)
    k1_low, k1_owner = grid(K_ONE, NX // 2)
    k1 = k1_owner * K_ONE + k1_low
    first = joined(*[table(k1, yes(k1), n, yes(n), -1.0, 1.0) for n in (n1[0::2], n1[1::2])])
    k2_low, k2_owner = grid(K_TWO, NY // 2)
    k2 = k2_owner * K_TWO + k2_low
    k3 = np.arange(LENGTH // 2)
    wholes = []
    for k, window, owners, wide in ((k2, WIN_ONE, NX, WIDE_ONE), (k3, WIN_TWO, NY, WIDE_TWO)):
        out, back = [], []
        for parity in range(2):
            cell, owner = grid(len(cells_of(window, parity)), owners)
            n, n_ok = window_index(owner, 2 * cell + 1 - parity, wide)
            out.append(table(k, yes(k), n, n_ok, -1.0, 1.0))
            back.append(table(n, n_ok, k, yes(k), 1.0, 1.0 / LENGTH))
        wholes.append((joined(*out), np.concatenate(back, axis=0)))
    return first, wholes[0][0], wholes[1][0], wholes[1][1], wholes[0][1], first_back


def split(value):
    high = value.astype(bf16)
    return high, (value - high.astype(f32)).astype(bf16)


def dot(left, right, dims=((1,), (0,))):
    return lax.dot_general(left, right, (dims, ((), ())), preferred_element_type=f32)


def transform(table, real, imag):
    high, low = split(jnp.concatenate([real, imag], axis=1))
    data = jnp.concatenate([high, high, low], axis=0)
    rows = table.shape[0] // 2
    cos, sin = dot(table[:rows], data), dot(table[rows:], data)
    return cos[:, :LANES] - sin[:, LANES:], cos[:, LANES:] + sin[:, :LANES]


def transform_cells(table_ref, cells):
    results = []
    for parity, parts in enumerate(cells):
        depth = 3 * parts[0].shape[0]
        start = 0 if parity else table_ref.shape[1] - depth
        results.append(transform(table_ref[:, start : start + depth], *parts))
    return [(even + odd, even - odd) for even, odd in zip(*results)]


def transform_window(table_ref, parts):
    return transform_cells(
        table_ref,
        [
            [jnp.concatenate([rows[place] for place in cells_of(len(rows), parity)], axis=0) for rows in parts]
            for parity in range(2)
        ],
    )


def by_owner(halves, owners, count):
    half = owners // 2
    return [
        jnp.concatenate([columns[low * half : (low + 1) * half] for columns in halves], axis=0) for low in range(count)
    ]


def window_transform(table_ref, parts, window, owners):
    rows = [[None] * window for _ in parts]
    start = 0
    for parity in range(2):
        places = cells_of(window, parity)
        data = [low - high if parity else low + high for low, high in parts]
        end = start + 2 * len(places) * owners
        for part, columns in enumerate(transform(table_ref[start:end], *data)):
            for at, place in enumerate(places):
                rows[part][place] = columns[at * owners : (at + 1) * owners]
        start = end
    return rows


def exchange_turned(arrays, block, count):
    shape = arrays[0].shape
    place = lax.broadcasted_iota(jnp.int32, shape, 1) // block
    arrays = [pltpu.roll(array, index * block, 1) if index else array for index, array in enumerate(arrays)]
    arrays += [jnp.zeros(shape, f32)] * (count - len(arrays))
    step = 1
    while step < count:
        odd = (place // step) % 2 == 1
        arrays = [jnp.where(odd, arrays[(index + step) % count], arrays[index]) for index in range(count)]
        step *= 2
    return [
        pltpu.roll(arrays[count - index], LANES - index * block, 1) if index else arrays[0] for index in range(count)
    ]


def exchange(arrays, block):
    lane = lax.broadcasted_iota(jnp.int32, arrays[0].shape, 1)
    step = 1
    while step < len(arrays):
        width = step * block
        low = (lane // width) % 2 == 0
        mixed = list(arrays)
        for place in range(len(arrays)):
            if place & step:
                continue
            first, second = arrays[place], arrays[place | step]
            mixed[place] = jnp.where(low, first, pltpu.roll(second, width, 1))
            mixed[place | step] = jnp.where(low, pltpu.roll(first, LANES - width, 1), second)
        arrays = mixed
        step *= 2
    return arrays


def lane_cell(shape):
    return lax.broadcasted_iota(jnp.int32, shape, 1) % PAD_TWO


def pack(rows):
    cell = lane_cell(rows[0].shape)
    message = list(rows[:ROWS_X])
    for extra, row in enumerate(rows[ROWS_X:]):
        for half in range(2):
            moved = pltpu.roll(row, WIN_TWO - half * HALF, 1)
            place = 2 * extra + half
            message[place] = jnp.where(cell >= WIN_TWO, moved, message[place])
        place = 2 * EXTRA_X
        message[place] = jnp.where(cell == WIN_TWO + extra, pltpu.roll(row, 1 + extra, 1), message[place])
    return message


def unpack(message):
    cell = lane_cell(message[0].shape)
    rows = []
    for extra in range(EXTRA_X):
        row = pltpu.roll(message[2 * EXTRA_X], LANES - 1 - extra, 1)
        for half in (1, 0):
            moved = pltpu.roll(message[2 * extra + half], LANES - WIN_TWO + half * HALF, 1)
            row = jnp.where(cell < (half + 1) * HALF, moved, row)
        rows.append(row)
    return rows


def gather(ref, row, count, stride):
    return ref[pl.ds(row, count, stride=stride), :]


def live_slots(count_ref, shape):
    slot = lax.broadcasted_iota(jnp.int32, shape, 0)
    limit = jnp.zeros(shape, jnp.int32)
    for index in range(shape[0]):
        limit = jnp.where(slot == index, count_ref[0, 0, index], limit)
    return lax.broadcasted_iota(jnp.int32, shape, 1) < limit


def cubic_taps(fraction):
    frac_sq = fraction * fraction
    frac_cube = frac_sq * fraction
    return (
        -0.5 * frac_cube + frac_sq - 0.5 * fraction,
        1.5 * frac_cube - 2.5 * frac_sq + 1.0,
        -1.5 * frac_cube + 2.0 * frac_sq + 0.5 * fraction,
        0.5 * frac_cube - 0.5 * frac_sq,
    )


def stencil(first, taps, slot, extent):
    first_row = first[slot : slot + 1]
    offset = lax.broadcasted_iota(jnp.int32, (extent, first.shape[1]), 0) - first_row
    result = jnp.zeros(offset.shape, f32)
    for index in range(4):
        result = jnp.where(offset == index, taps[index][slot : slot + 1], result)
    return result


def point_weights(cells_ref, fracs_ref):
    firsts = [cells_ref[dim, 0, 0] & (wide - 1) for dim, wide in enumerate((TL, WIDE_ONE, WIDE_TWO))]
    taps = [cubic_taps(fracs_ref[dim, 0, 0]) for dim in range(3)]

    def weights(slot):
        depth = stencil(firsts[0], taps[0], slot, SPAN)
        across = stencil(firsts[1], taps[1], slot, PAD_ONE)
        upward = stencil(firsts[2], taps[2], slot, PAD_TWO)
        plane = across[:WIN_ONE, None, :] * upward[None, :, :]
        return depth, plane.reshape(WIN_ONE * PAD_TWO, plane.shape[2])

    return weights


def spread_kernel(*refs):
    outside, refs = refs[:6], refs[6:]
    out_ref, masked_ref, live_ref, depth_ref, plane_ref, near_tile_ref, *inside, win_ref, sems = refs
    tile_ref, count_ref, dir_ref, cells_ref, fracs_ref, table_ref = inside
    copies = [pltpu.make_async_copy(far, near, sems.at[at]) for at, (far, near) in enumerate(zip(outside, inside))]
    copies.append(pltpu.make_async_copy(outside[0], near_tile_ref, sems.at[len(copies)]))
    for copy in copies:
        copy.start()
    win_ref[...] = jnp.zeros_like(win_ref)
    for copy in copies[:5]:
        copy.wait()
    probes, slots = dir_ref.shape[0], dir_ref.shape[3]
    live = live_slots(count_ref, dir_ref.shape[3:])
    live_ref[...] = live.astype(f32)
    masked = [jnp.where(live, dir_ref[probe, 0, 0], 0.0) for probe in range(probes)]
    for probe in range(probes):
        masked_ref[probe] = masked[probe]
    weights = point_weights(cells_ref, fracs_ref)
    for slot in range(slots):
        depth, plane = weights(slot)
        high, low = split(plane)
        rest = jnp.zeros((LANES - plane.shape[0], plane.shape[1]), bf16)
        planes = jnp.concatenate([high, rest, low, rest], axis=0)
        depth_ref[slot], plane_ref[slot] = depth, planes
        values = jnp.concatenate([depth * masked[probe][slot : slot + 1] for probe in range(probes)], axis=0)
        rows = values.shape[0]
        both = dot(jnp.concatenate(split(values), axis=0), planes, ((1,), (1,)))
        total = both[:rows, :LANES] + (both[:rows, LANES:] + both[rows:, :LANES])
        place = pl.ds(pl.multiple_of(tile_ref[0, 0, slot] * TL, TL), SPAN)
        for probe in range(probes):
            win_ref[probe, place, :] += total[probe * SPAN : (probe + 1) * SPAN]
    for copy in copies[5:]:
        copy.wait()
    cells = [[win_ref[probe, pl.ds(1 + parity, G // 2, stride=2), :] for probe in range(probes)] for parity in range(2)]
    rows = []
    for halves in transform_cells(table_ref, cells):
        pieces = by_owner(halves, NX, K_ONE)
        rows += exchange(pieces, PAD_TWO)[:WIN_ONE]
    for row, piece in enumerate(pack(rows)):
        out_ref[pl.ds(row, NX, stride=ROWS_X), :] = piece


def window_rows(in_ref):
    rows = [gather(in_ref, row, NX, ROWS_X) for row in range(ROWS_X)]
    return rows + unpack(rows)


def second_kernel(in_ref, table_ref, out_ref):
    rows = window_rows(in_ref)
    parts = transform_window(table_ref, [rows[:WIN_ONE], rows[WIN_ONE:]])
    for part, halves in enumerate(parts):
        pieces = by_owner(halves, NY, K_TWO)
        for cell, piece in enumerate(exchange_turned(pieces, 1, PAD_TWO)[:WIN_TWO]):
            out_ref[pl.ds(2 * cell + part, NY, stride=ROWS_Y), :] = piece


def third_kernel(in_ref, spec_ref, table_ref, back_ref, out_ref):
    parts = [[gather(in_ref, 2 * cell + part, NY, ROWS_Y) for cell in range(WIN_TWO)] for part in range(2)]
    factor = spec_ref[...].reshape(LANES, LENGTH).T
    factors = factor[:G], factor[G:]
    scaled = [
        [columns * factor for columns, factor in zip(halves, factors)]
        for halves in transform_window(table_ref, parts)
    ]
    for part, rows in enumerate(window_transform(back_ref, scaled, WIN_TWO, NY)):
        for cell, row in enumerate(rows):
            out_ref[pl.ds(2 * cell + part, NY, stride=ROWS_Y), :] = row


def fourth_kernel(in_ref, table_ref, out_ref):
    parts = []
    half = NY // 2
    for part in range(2):
        pieces = [gather(in_ref, 2 * cell + part, NY, ROWS_Y) for cell in range(WIN_TWO)]
        pieces = exchange_turned(pieces, 1, K_TWO)
        parts.append([jnp.concatenate([piece[at : at + half] for piece in pieces], axis=0) for at in (0, half)])
    rows = sum(window_transform(table_ref, parts, WIN_ONE, NX), [])
    for row, piece in enumerate(pack(rows)):
        out_ref[pl.ds(row, NX, stride=ROWS_X), :] = piece


def read_kernel(
    near_tile_ref, in_ref, res_ref, dir_ref, live_ref, depth_ref, plane_ref, table_ref,
    image_ref, sums_ref, win_ref,
):
    tile_row = near_tile_ref[0]
    own = lax.broadcasted_iota(jnp.int32, tile_row.shape, 1)
    tiles = [jnp.max(jnp.where(own == slot, tile_row, 0)) for slot in range(tile_row.shape[1])]
    probes, slots = image_ref.shape[:2]
    rows = window_rows(in_ref)
    parts = []
    for part in range(2):
        pieces = rows[part * WIN_ONE : (part + 1) * WIN_ONE]
        parts.append(jnp.concatenate(exchange_turned(pieces, PAD_TWO, K_ONE), axis=0))
    smooth = transform(table_ref[...], *parts)
    win_ref[...] = jnp.zeros_like(win_ref)
    for probe in range(probes):
        win_ref[probe, 1 : G + 1, :] = smooth[probe]
    for slot in range(slots):
        place = pl.ds(pl.multiple_of(tiles[slot] * TL, TL), SPAN)
        block = jnp.concatenate([win_ref[probe, place, :] for probe in range(probes)], axis=0)
        block_high, block_low = split(block)
        rows = block.shape[0]
        left = jnp.concatenate([block_high, block_low], axis=0)
        right = jnp.concatenate([block_high, jnp.zeros_like(block_low)], axis=0)
        both = dot(jnp.concatenate([left, right], axis=1), plane_ref[slot])
        total = both[:rows] + both[rows:]
        for probe in range(probes):
            image_ref[probe, slot : slot + 1, :] = jnp.sum(
                depth_ref[slot] * total[probe * SPAN : (probe + 1) * SPAN], axis=0, keepdims=True
            )
    sums = []
    live = live_ref[...]
    for probe in range(probes):
        masked_res, masked_dir = live * res_ref[probe, 0, 0], dir_ref[probe]
        image = live * image_ref[probe] + NOISE * masked_dir
        image_ref[probe] = image
        for left, right in (
            (masked_res, masked_res),
            (masked_dir, image),
            (masked_res, image),
            (image, image),
        ):
            line = jnp.sum(left * right, axis=0, keepdims=True)
            sums.append(sum(line[:, at : at + LANES] for at in range(0, line.shape[1], LANES)))
    column = jnp.sum(jnp.concatenate(sums, axis=0), axis=1, keepdims=True)
    shape = (column.shape[0], LANES)
    own = lax.broadcasted_iota(jnp.int32, shape, 0) == lax.broadcasted_iota(jnp.int32, shape, 1)
    row = jnp.sum(jnp.where(own, column, 0.0), axis=0, keepdims=True)
    sums_ref[...] = jnp.broadcast_to(row, sums_ref.shape)


def total_kernel(in_ref, out_ref):
    out_ref[...] = jnp.broadcast_to(jnp.sum(in_ref[...], axis=0, keepdims=True), out_ref.shape)


def update_kernel(
    sums_ref, image_ref, live_ref, iterate_ref, res_ref, dir_ref, new_iterate_ref, new_res_ref, new_dir_ref
):
    sums = jnp.sum(sums_ref[...], axis=0, keepdims=True)
    live = live_ref[...]
    for probe in range(image_ref.shape[0]):
        old_norm, curvature, crossed, squared = (sums[:, 4 * probe + at : 4 * probe + at + 1] for at in range(4))
        alpha = old_norm / curvature
        new_norm = old_norm + alpha * (alpha * squared - 2.0 * crossed)
        beta = new_norm / old_norm
        masked_dir = dir_ref[probe]
        new_res = live * res_ref[probe, 0, 0] - alpha * image_ref[probe]
        new_iterate_ref[probe, 0, 0] = live * iterate_ref[probe, 0, 0] + alpha * masked_dir
        new_res_ref[probe, 0, 0] = new_res
        new_dir_ref[probe, 0, 0] = new_res + beta * masked_dir


def call(kernel, name, outs, operands, far=0, scratch=(), cost=None):
    operands = [pltpu.with_memory_space_constraint(operand, pltpu.HBM) for operand in operands[:far]] + [*operands[far:]]
    near = len(operands) - far
    outs = [jax.ShapeDtypeStruct(*(out if isinstance(out[0], tuple) else (out, f32))) for out in outs]
    return pl.pallas_call(
        kernel,
        out_shape=outs,
        in_specs=[pl.BlockSpec(memory_space=pltpu.HBM)] * far + [pl.BlockSpec(memory_space=pltpu.VMEM)] * near,
        out_specs=[pl.BlockSpec(memory_space=pltpu.VMEM)] * len(outs),
        scratch_shapes=list(scratch),
        compiler_params=pltpu.CompilerParams(vmem_limit_bytes=VMEM_LIMIT),
        cost_estimate=cost,
        name=name,
    )(*operands)


def across(axis, value):
    rows = value.shape[0]
    sent = value.reshape(rows, 1, LANES)
    return lax.all_to_all(sent, axis, split_axis=0, concat_axis=0, tiled=True).reshape(rows, LANES)


def on_device(iterate, residual, direction, cells, fracs, counts, slot_tile, spectrum):
    first, second, third, third_back, second_back, first_back = tables()
    probes, slots, cap = direction.shape[0], direction.shape[3], direction.shape[4]
    window = pltpu.VMEM((probes, WIN_ROWS, LANES), f32)
    operands = (slot_tile, counts, direction, cells, fracs, first)
    near = [
        (pltpu.SMEM if at < 2 else pltpu.VMEM)(operand.shape, operand.dtype) for at, operand in enumerate(operands)
    ]
    sent, masked, live, depth, planes, near_tile = call(
        spread_kernel,
        "spread",
        [
            (NX * ROWS_X, LANES),
            (probes, slots, cap),
            (slots, cap),
            (slots, SPAN, cap),
            ((slots, 2 * LANES, cap), bf16),
            (slot_tile.shape, slot_tile.dtype),
        ],
        operands,
        far=len(operands),
        cost=pl.CostEstimate(flops=4_000_000_000, bytes_accessed=24_000_000, transcendentals=0),
        scratch=(*near, window, pltpu.SemaphoreType.DMA((len(operands) + 1,))),
    )
    came = across("gx", sent)
    (sent,) = call(second_kernel, "second", [(NY * ROWS_Y, LANES)], (came, second))
    came = across("gy", sent)
    (sent,) = call(third_kernel, "third", [(NY * ROWS_Y, LANES)], (came, spectrum, third, third_back))
    came = across("gy", sent)
    (sent,) = call(fourth_kernel, "fourth", [(NX * ROWS_X, LANES)], (came, second_back))
    came = across("gx", sent)
    image, sums = call(
        read_kernel,
        "read",
        [(probes, slots, cap), (NY, LANES)],
        (near_tile, came, residual, masked, live, depth, planes, first_back),
        scratch=(window,),
    )
    sums = across("gy", sums)
    (sums,) = call(total_kernel, "total", [(NX, LANES)], (sums,))
    sums = across("gx", sums)
    return tuple(call(update_kernel, "update", [direction.shape] * 3, (sums, image, live, iterate, residual, masked)))


def solution(mesh):
    points = P(None, "gx", "gy", None, None)
    blocks = P("gx", "gy", None)
    return jax.shard_map(
        on_device,
        mesh=mesh,
        in_specs=(points, points, points, points, points, blocks, blocks, blocks),
        out_specs=(points, points, points),
        check_vma=False,
    )
```
